32 devices in a mesh: section: 2 (over x), tensor: 4 (over y, core), dp: 4 (over z).
Axes of the slice: x: 2, y: 2, z: 4, core: 2. Of those that a mesh axis runs over, the one named last changes fastest.
Arguments:
- tokens: bfloat16 [8, 256, 1152], P('dp')
- cotangent: bfloat16 [8, 256, 1152], P('dp'), may hold values from -6 to 6
- kept_index: int32 [8, 256], P('dp'), may hold values from 0 to 255, as said below
- full_flag: int32 [8], P('dp'), may hold values 0 or 1
- labels: int32 [8], P('dp'), may hold values from 0 to 999
- timesteps: int32 [8], P('dp'), may hold values from 0 to 999
- class_table: bfloat16 [1000, 1152], replicated, may hold values from -6 to 6
- heads_weight: float32 [2, 3, 1152, 1152], P('section', None, 'dp', 'tensor')
- heads_first: float32 [2, 3, 1152, 1152], P('section', None, 'dp', 'tensor'), may hold values from -0.00024414062 to 0.00024414062
- heads_second: float32 [2, 3, 1152, 1152], P('section', None, 'dp', 'tensor'), may hold values from 2.1139925e-10 to 8.45597e-10
- output_weight: float32 [2, 1152, 1152], P('section', 'tensor', 'dp'), may hold values from -0.75 to 0.75
- output_first: float32 [2, 1152, 1152], P('section', 'tensor', 'dp'), may hold values from -0.00024414062 to 0.00024414062
- output_second: float32 [2, 1152, 1152], P('section', 'tensor', 'dp'), may hold values from 2.1139925e-10 to 8.45597e-10
- up_weight: float32 [2, 1152, 4608], P('section', 'dp', 'tensor')
- up_first: float32 [2, 1152, 4608], P('section', 'dp', 'tensor'), may hold values from -4.5776367e-05 to 4.5776367e-05
- up_second: float32 [2, 1152, 4608], P('section', 'dp', 'tensor'), may hold values from 8.45597e-12 to 3.382388e-11
- down_weight: float32 [2, 4608, 1152], P('section', 'tensor', 'dp'), may hold values from -0.09375 to 0.09375
- down_first: float32 [2, 4608, 1152], P('section', 'tensor', 'dp'), may hold values from -0.00024414062 to 0.00024414062
- down_second: float32 [2, 4608, 1152], P('section', 'tensor', 'dp'), may hold values from 2.1139925e-10 to 8.45597e-10
- adaln_weight: float32 [2, 1152, 6912], P('section', 'dp', 'tensor'), may hold values from -0.1875 to 0.1875
- adaln_first: float32 [2, 1152, 6912], P('section', 'dp', 'tensor'), may hold values from -0.00024414062 to 0.00024414062
- adaln_second: float32 [2, 1152, 6912], P('section', 'dp', 'tensor'), may hold values from 2.1139925e-10 to 8.45597e-10
- mask_token: float32 [1152], replicated, may hold values from -1.25 to 1.25
- mask_first: float32 [1152], replicated, may hold values from -0.0014648438 to 0.0014648438
- mask_second: float32 [1152], replicated, may hold values from 7.618746e-09 to 3.043312e-08
Outputs:
- block_outputs: bfloat16 [2, 8, 256, 1152], P('section', 'dp')
- input_grads: bfloat16 [2, 8, 256, 1152], P('section', 'dp')
- heads_weight_next: float32 [2, 3, 1152, 1152], P('section', None, 'dp', 'tensor')
- heads_first_next: float32 [2, 3, 1152, 1152], P('section', None, 'dp', 'tensor')
- heads_second_next: float32 [2, 3, 1152, 1152], P('section', None, 'dp', 'tensor')
- output_weight_next: float32 [2, 1152, 1152], P('section', 'tensor', 'dp')
- output_first_next: float32 [2, 1152, 1152], P('section', 'tensor', 'dp')
- output_second_next: float32 [2, 1152, 1152], P('section', 'tensor', 'dp')
- up_weight_next: float32 [2, 1152, 4608], P('section', 'dp', 'tensor')
- up_first_next: float32 [2, 1152, 4608], P('section', 'dp', 'tensor')
- up_second_next: float32 [2, 1152, 4608], P('section', 'dp', 'tensor')
- down_weight_next: float32 [2, 4608, 1152], P('section', 'tensor', 'dp')
- down_first_next: float32 [2, 4608, 1152], P('section', 'tensor', 'dp')
- down_second_next: float32 [2, 4608, 1152], P('section', 'tensor', 'dp')
- adaln_weight_next: float32 [2, 1152, 6912], P('section', 'dp', 'tensor')
- adaln_first_next: float32 [2, 1152, 6912], P('section', 'dp', 'tensor')
- adaln_second_next: float32 [2, 1152, 6912], P('section', 'dp', 'tensor')
- mask_token_next: float32 [1152], replicated
- mask_first_next: float32 [1152], replicated
- mask_second_next: float32 [1152], replicated
- grad_norm: float32 [], replicated
The draws below stay inside these ranges and needn't reach their ends.
Inputs may be any that keep to these rules, and one draw needn't show every extreme that they name: `kept_index`: each row is a permutation of 0 to 255; an image keeps the tokens named by its first 128 entries, or all of them where its flag is 1.
All inputs are finite; a program needn't handle non-finite values. No bound on the sum of `full_flag` on one device may be relied on, other than what follows from the above.
Results may differ from the reference program's by a relative error of at most 0.025.
Values may be sent and summed in bfloat16 or wider, within the bound.
No kernel may reach another device: no remote copies, remote signals or barrier semaphores. Data moves between devices by JAX's collectives and lax.ppermute only.
A program may use at most 192 MiB of HBM per device.

```python
import math
import jax
import jax.numpy as jnp
from jax import lax

D = 1152
HEADS = 16
HEAD_DIM = 72
FF = 4608
CLASSES = 1000
S = 256
STEP = 10
IMG_DEV = 2
IMAGES = 8


def rising(length, top):
    return 1.0 + (top - 1.0) * jnp.arange(length, dtype=jnp.float32) / (length - 1)


def draw_tokens(key, part):
    key = jax.random.fold_in(key, 11)
    values = jax.random.normal(key, (IMAGES, S, D), jnp.float32) * rising(D, 3.0)[None, None, :]
    return values.astype(jnp.bfloat16)


def draw_kept_index(key, part):
    key = jax.random.fold_in(key, 12)
    row_keys = jax.random.split(key, IMAGES)
    return jax.vmap(lambda row_key: jax.random.permutation(row_key, S))(row_keys).astype(jnp.int32)


def draw_heads_weight(key, part):
    key = jax.random.fold_in(key, 13)
    values = jax.random.normal(key, (2, 3, D, D), jnp.float32)
    ramped = rising(D, 3.0)
    ones_row = jnp.ones((D,), jnp.float32)
    factor = jnp.stack([ones_row, ones_row, ramped])[None, :, None, :]
    return values * factor * D ** (-0.5)


def draw_up_weight(key, part):
    key = jax.random.fold_in(key, 14)
    values = jax.random.normal(key, (2, D, FF), jnp.float32) * rising(FF, 3.0)[None, None, :]
    return values * D ** (-0.5)


def place_ends(array, stream_key, smallest, top_value):
    extent = array.shape
    index_at = [jax.random.randint(jax.random.fold_in(stream_key, axis), (), 0, extent[axis]) for axis in range(len(extent))]
    array = array.at[tuple(index_at)].set(smallest)
    longest = extent.index(max(extent))
    index_at[longest] = (index_at[longest] + 1) % extent[longest]
    return array.at[tuple(index_at)].set(top_value)


def steps_of(own_key, shape, shards, low, high):
    def one(axis_at, parts):
        heights = jax.random.uniform(jax.random.fold_in(jax.random.fold_in(own_key, 6), axis_at), (parts,), jnp.float32, low / len(shards), high / len(shards))
        return jnp.repeat(jnp.exp(heights), shape[axis_at] // parts).reshape((-1,) + (1,) * (len(shape) - axis_at - 1))

    level = one(*shards[0])
    for cut in shards[1:]:
        level = level * one(*cut)
    return level


def gaussian(rng, extent, scale, limit, cuts=(), held_as=jnp.bfloat16):
    loudness = steps_of(rng, extent, cuts, -0.22, 0.18) if cuts else 1.0
    array = jax.random.normal(rng, extent, jnp.float32) * scale * loudness
    return jnp.minimum(jnp.maximum(array, -limit), limit).astype(held_as)


def setup_inputs(seed: int = 0) -> dict:
    key_of = jax.random.split(jax.random.key(seed), 26)
    return {
        "tokens": draw_tokens(jax.random.fold_in(key_of[25], 71), 0),
        "cotangent": gaussian(key_of[1], (IMAGES, S, D), 1.0, 6.0, ((0, 4),)),
        "kept_index": draw_kept_index(jax.random.fold_in(key_of[25], 71), 0),
        "full_flag": place_ends((jax.random.randint(key_of[3], (IMAGES,), 0, 4) < 1).astype(jnp.int32), jax.random.fold_in(key_of[3], 1), 0, 1),
        "labels": place_ends(jax.random.randint(key_of[4], (IMAGES,), 0, CLASSES), jax.random.fold_in(key_of[4], 1), 0, CLASSES - 1).astype(jnp.int32),
        "timesteps": place_ends(jax.random.randint(key_of[5], (IMAGES,), 0, 1000), jax.random.fold_in(key_of[5], 1), 0, 999).astype(jnp.int32),
        "class_table": gaussian(key_of[6], (CLASSES, D), 1.0, 6.0),
        "heads_weight": draw_heads_weight(jax.random.fold_in(key_of[25], 71), 0),
        "heads_first": gaussian(key_of[8], (2, 3, D, D), (0.111 * (2 * (10 * D * D + 2 * D * FF) + D) ** -0.5), 0.00024414062, ((0, 2), (2, 4), (3, 4)), jnp.float32),
        "heads_second": jnp.clip(jnp.exp(math.log(8.455969813248032e-10) - 1.3862944 * jax.random.uniform(key_of[9], (2, 3, D, D), jnp.float32) ** steps_of(key_of[9], (2, 3, D, D), ((0, 2), (2, 4), (3, 4)), -0.2, 0.2)), 2.113992453312008e-10, 8.455969813248032e-10),
        "output_weight": gaussian(key_of[10], (2, D, D), (D // 16) ** -0.5, 0.75, ((0, 2), (1, 4), (2, 4)), jnp.float32),
        "output_first": gaussian(key_of[11], (2, D, D), (0.111 * (2 * (10 * D * D + 2 * D * FF) + D) ** -0.5), 0.00024414062, ((0, 2), (1, 4), (2, 4)), jnp.float32),
        "output_second": jnp.clip(jnp.exp(math.log(8.455969813248032e-10) - 1.3862944 * jax.random.uniform(key_of[12], (2, D, D), jnp.float32) ** steps_of(key_of[12], (2, D, D), ((0, 2), (1, 4), (2, 4)), -0.2, 0.2)), 2.113992453312008e-10, 8.455969813248032e-10),
        "up_weight": draw_up_weight(jax.random.fold_in(key_of[25], 71), 0),
        "up_first": gaussian(key_of[14], (2, D, FF), (0.0222 * (2 * (10 * D * D + 2 * D * FF) + D) ** -0.5), 4.57763671875e-05, ((0, 2), (1, 4), (2, 4)), jnp.float32),
        "up_second": jnp.clip(jnp.exp(math.log(3.382388119588242e-11) - 1.3862944 * jax.random.uniform(key_of[15], (2, D, FF), jnp.float32) ** steps_of(key_of[15], (2, D, FF), ((0, 2), (1, 4), (2, 4)), -0.2, 0.2)), 8.455970298970605e-12, 3.382388119588242e-11),
        "down_weight": gaussian(key_of[16], (2, FF, D), FF ** -0.5, 0.09375, ((0, 2), (1, 4), (2, 4)), jnp.float32),
        "down_first": gaussian(key_of[17], (2, FF, D), (0.111 * (2 * (10 * D * D + 2 * D * FF) + D) ** -0.5), 0.00024414062, ((0, 2), (1, 4), (2, 4)), jnp.float32),
        "down_second": jnp.clip(jnp.exp(math.log(8.455969813248032e-10) - 1.3862944 * jax.random.uniform(key_of[18], (2, FF, D), jnp.float32) ** steps_of(key_of[18], (2, FF, D), ((0, 2), (1, 4), (2, 4)), -0.2, 0.2)), 2.113992453312008e-10, 8.455969813248032e-10),
        "adaln_weight": gaussian(key_of[19], (2, D, 6 * D), D ** -0.5, 0.1875, ((0, 2), (1, 4), (2, 4)), jnp.float32),
        "adaln_first": gaussian(key_of[20], (2, D, 6 * D), (0.111 * (2 * (10 * D * D + 2 * D * FF) + D) ** -0.5), 0.00024414062, ((0, 2), (1, 4), (2, 4)), jnp.float32),
        "adaln_second": jnp.clip(jnp.exp(math.log(8.455969813248032e-10) - 1.3862944 * jax.random.uniform(key_of[21], (2, D, 6 * D), jnp.float32) ** steps_of(key_of[21], (2, D, 6 * D), ((0, 2), (1, 4), (2, 4)), -0.2, 0.2)), 2.113992453312008e-10, 8.455969813248032e-10),
        "mask_token": gaussian(key_of[22], (D,), 0.08, 1.25, (), jnp.float32),
        "mask_first": gaussian(key_of[23], (D,), (0.666 * (2 * (10 * D * D + 2 * D * FF) + D) ** -0.5), 0.0014648438, (), jnp.float32),
        "mask_second": jnp.clip(jnp.exp(jax.random.uniform(key_of[24], (D,), jnp.float32, math.log(7.61874563437459e-09), math.log(3.0433120912221057e-08))), 7.61874563437459e-09, 3.0433120912221057e-08),
    }


@jax.custom_vjp
def low(v):
    return lax.optimization_barrier(v.astype(jnp.bfloat16)).astype(jnp.float32)

@jax.custom_vjp
def low_back(v):
    return v

def low_keep(v):
    return (low(v), None)

def low_pass(kept, grad):
    return (grad,)

def back_keep(v):
    return (v, None)

def back_low(kept, grad):
    return (low(grad),)
low.defvjp(low_keep, low_pass)
low_back.defvjp(back_keep, back_low)
PRECISE = lax.Precision.HIGHEST
NORM_EPS = 1e-06
BETA_ONE = 0.9
BETA_TWO = 0.99
LEARN_RATE = 0.05
WEIGHT_DECAY = 0.01
ADAM_EPS = 1e-08
CLIP_NORM = 1.0
MASK_SCORE = -1000000000.0

def layer_norm(values):
    center = values - lax.optimization_barrier(jnp.mean(values, axis=-1, keepdims=True))
    spread = lax.optimization_barrier(jnp.mean(center * center, axis=-1, keepdims=True))
    return center * lax.rsqrt(spread + NORM_EPS)

def time_embed(steps_in, model_width):
    half_width = model_width // 2
    frequency = jnp.exp(-math.log(10000.0) * jnp.arange(half_width, dtype=jnp.float32) / half_width)
    angles = steps_in.astype(jnp.float32)[:, None] * frequency[None, :]
    return jnp.concatenate([jnp.cos(angles), jnp.sin(angles)], axis=-1)

def block(inputs, modulation, keys_live, w_heads, w_output, w_up, w_down):
    batch_size, seq_length, model_width = inputs.shape
    shift_a, scale_a, gate_a, shift_b, scale_b, gate_b = [modulation[:, position][:, None, :] for position in range(6)]
    normed = low(layer_norm(inputs) * (1.0 + scale_a) + shift_a)
    stacked = low(low_back(jnp.einsum('bsd,nde->nbse', normed, w_heads, precision=PRECISE)))
    by_head = stacked.reshape(3, batch_size, seq_length, HEADS, HEAD_DIM)
    scores = low_back(jnp.einsum('bqhe,bkhe->bhqk', by_head[0], by_head[1], precision=PRECISE) * HEAD_DIM ** (-0.5))
    scores = jnp.where(keys_live[:, None, None, :] > 0, scores, MASK_SCORE)
    probability = low(jax.nn.softmax(scores, axis=-1))
    attended = low(low_back(jnp.einsum('bhqk,bkhe->bqhe', probability, by_head[2], precision=PRECISE)))
    attended = attended.reshape(batch_size, seq_length, model_width)
    branch_a = low_back(jnp.einsum('bsd,de->bse', attended, w_output, precision=PRECISE))
    hidden = inputs + gate_a * branch_a
    normed_b = low(layer_norm(hidden) * (1.0 + scale_b) + shift_b)
    up_value = low_back(jnp.einsum('bsd,df->bsf', normed_b, w_up, precision=PRECISE))
    activated = low(jax.nn.gelu(up_value, approximate=True))
    branch_b = low_back(jnp.einsum('bsf,fd->bsd', activated, w_down, precision=PRECISE))
    return hidden + gate_b * branch_b

def forward(params, tokens_in, probe_zero, placement, slot_live, covered, cond_act):
    heads_weight, output_weight, up_weight, down_weight, adaln_weight, mask_token = params
    model_width = tokens_in.shape[-1]

    def layer_mod(layer):
        return jnp.einsum('bd,de->be', cond_act, low(adaln_weight[layer]), precision=PRECISE).reshape(-1, 6, model_width)
    enc_in = jnp.einsum('bst,btd->bsd', placement, tokens_in, precision=PRECISE)
    enc_out = block(enc_in, layer_mod(0), slot_live, low(heads_weight[0]), low(output_weight[0]), low(up_weight[0]), low(down_weight[0])) * slot_live[:, :, None]
    sent_rows = low_back(low(enc_out))
    dec_in = jnp.einsum('bst,bsd->btd', placement, sent_rows, precision=PRECISE)
    dec_in = dec_in + (1.0 - covered)[:, :, None] * mask_token[None, None, :] + probe_zero
    dec_out = block(dec_in, layer_mod(1), jnp.ones_like(slot_live), low(heads_weight[1]), low(output_weight[1]), low(up_weight[1]), low(down_weight[1]))
    return (enc_out, dec_out)

def adam_update(weight_in, first_in, second_in, gradient, factor):
    clipped = gradient * factor
    first_out = BETA_ONE * first_in + (1.0 - BETA_ONE) * clipped
    second_out = BETA_TWO * second_in + (1.0 - BETA_TWO) * clipped * clipped
    ratio = first_out / (1.0 - BETA_ONE ** STEP) / (jnp.sqrt(second_out / (1.0 - BETA_TWO ** STEP)) + ADAM_EPS)
    weight_out = weight_in - LEARN_RATE * (ratio + WEIGHT_DECAY * weight_in)
    return (weight_out, first_out, second_out)

def reference(tokens, cotangent, kept_index, full_flag, labels, timesteps, class_table, heads_weight, heads_first, heads_second, output_weight, output_first, output_second, up_weight, up_first, up_second, down_weight, down_first, down_second, adaln_weight, adaln_first, adaln_second, mask_token, mask_first, mask_second):
    image_count, seq_length, model_width = tokens.shape
    slot_ids = jnp.arange(seq_length, dtype=jnp.int32)
    counts = jnp.where(full_flag > 0, seq_length, seq_length // 2).astype(jnp.int32)
    slot_live = (slot_ids[None, :] < counts[:, None]).astype(jnp.float32)
    placement = (kept_index[:, :, None] == slot_ids[None, None, :]).astype(jnp.float32) * slot_live[:, :, None]
    covered = lax.optimization_barrier(jnp.sum(placement, axis=1))
    condition = class_table.astype(jnp.float32)[labels] + time_embed(timesteps, model_width)
    cond_act = low(jax.nn.silu(condition))
    group_count = image_count // IMG_DEV

    def by_group(values):
        return values.reshape((group_count, IMG_DEV) + values.shape[1:])
    params = (heads_weight, output_weight, up_weight, down_weight, adaln_weight, mask_token)
    zero_grads = jax.tree.map(jnp.zeros_like, params)

    def one_group(grad_total, group_item):
        tokens_part, cot_part, place_part, live_part, cover_part, cond_part = group_item

        def run(params_in, tokens_in, probe_zero):
            return forward(params_in, tokens_in, probe_zero, place_part, live_part, cover_part, cond_part)
        outs, pullback = jax.vjp(run, params, tokens_part.astype(jnp.float32), jnp.zeros(tokens_part.shape, jnp.float32))
        grads, tokens_grad, probe_grad = pullback((jnp.zeros_like(outs[0]), cot_part.astype(jnp.float32)))
        grad_total = jax.tree.map(jnp.add, grad_total, grads)
        return (grad_total, (outs[0].astype(jnp.bfloat16), outs[1].astype(jnp.bfloat16), tokens_grad.astype(jnp.bfloat16), probe_grad.astype(jnp.bfloat16)))
    grad_total, (enc_rows, dec_rows, tokens_grad, probe_grad) = lax.scan(one_group, zero_grads, (by_group(tokens), by_group(cotangent), by_group(placement), by_group(slot_live), by_group(covered), by_group(cond_act)))
    full_shape = (image_count, seq_length, model_width)
    block_outputs = jnp.stack([enc_rows.reshape(full_shape), dec_rows.reshape(full_shape)])
    input_grads = jnp.stack([tokens_grad.reshape(full_shape), probe_grad.reshape(full_shape)])
    squared = sum((jnp.sum(gradient * gradient) for gradient in grad_total))
    grad_norm = jnp.sqrt(squared)
    factor = jnp.minimum(1.0, CLIP_NORM / (grad_norm + NORM_EPS))
    firsts = (heads_first, output_first, up_first, down_first, adaln_first, mask_first)
    seconds = (heads_second, output_second, up_second, down_second, adaln_second, mask_second)
    updated = [adam_update(params[position], firsts[position], seconds[position], grad_total[position], factor) for position in range(6)]
    return (block_outputs, input_grads, updated[0][0], updated[0][1], updated[0][2], updated[1][0], updated[1][1], updated[1][2], updated[2][0], updated[2][1], updated[2][2], updated[3][0], updated[3][1], updated[3][2], updated[4][0], updated[4][1], updated[4][2], updated[5][0], updated[5][1], updated[5][2], grad_norm)
```

```python
import math

import jax
import jax.numpy as jnp
from jax import lax
from jax.sharding import Mesh
from jax.sharding import PartitionSpec as P

HEAD_DIM = 72
STEP = 10

PRECISE = lax.Precision.HIGHEST
NORM_EPS = 1e-06
BETA_ONE = 0.9
BETA_TWO = 0.99
LEARN_RATE = 0.05
WEIGHT_DECAY = 0.01
ADAM_EPS = 1e-08
CLIP_NORM = 1.0
MASK_SCORE = -1000000000.0

BF = jnp.bfloat16
F32 = jnp.float32
PLANE = ("section", "row", "core")
CHIPS = ("section", "row")
ROWS_BY = ("dp", "core")


def dot(left, right, dims, out=F32):
    return lax.dot_general(left, right, (dims, ((), ())), preferred_element_type=F32).astype(out)


def mm(left, right, out=F32):
    return dot(left, right, ((1,), (0,)), out)


def mm_nt(left, right, out=F32):
    return dot(left, right, ((1,), (1,)), out)


def mm_tn(left, right, out=F32):
    return dot(left, right, ((0,), (0,)), out)


def chip_route(offset):
    return [
        (s * 2 + r, (s ^ (offset & 1)) * 2 + (r ^ (offset >> 1)))
        for s in range(2)
        for r in range(2)
    ]


def swap_chips(block, offset):
    return lax.ppermute(block, CHIPS, chip_route(offset))


def swap_cores(block):
    return lax.ppermute(block, "core", [(0, 1), (1, 0)])


def gather_rows(own):
    return jnp.concatenate([own] + [swap_chips(own, offset) for offset in (1, 2, 3)], axis=0)


def sum_rows(partial):
    count = partial.shape[0] // 4
    low = partial.astype(BF)
    total = partial[:count]
    for offset in (1, 2, 3):
        total = total + swap_chips(low[offset * count : (offset + 1) * count], offset).astype(F32)
    return total


def xor_route(size, offset):
    return [(i, i ^ offset) for i in range(size)]


def planes_gather(block):
    size = lax.axis_size("dp")
    parts = [block] + [
        lax.ppermute(block, "dp", xor_route(size, offset)) for offset in range(1, size)
    ]
    return jnp.concatenate(parts, axis=0)


def planes_sum(blocks):
    size = lax.axis_size("dp")
    count = blocks.shape[0] // size
    total = blocks[:count]
    for offset in range(1, size):
        part = blocks[offset * count : (offset + 1) * count]
        total = total + lax.ppermute(part, "dp", xor_route(size, offset))
    return total


def sum_everywhere(values):
    for axis in ("core", "section", "row", "dp"):
        size = lax.axis_size(axis)
        step = 1
        while step < size:
            values = values + lax.ppermute(values, axis, xor_route(size, step))
            step *= 2
    return values


def plane_index(section, core):
    return section * 2 + core


def send_shares(pack, section):
    half = pack.shape[0] // 2
    cases = [(s, c) for s in range(2) for c in range(2)]
    same = lax.dynamic_slice_in_dim(pack, section * half, half, 0)
    other = lax.dynamic_slice_in_dim(pack, (1 - section) * half, half, 0)
    axes = ("section", "core")
    same = lax.ppermute(same, axes, [(s * 2 + c, c * 2 + s) for s, c in cases])
    other = lax.ppermute(other, axes, [(s * 2 + c, c * 2 + 1 - s) for s, c in cases])
    return (same, other)


def return_shares(first, second, section, core):
    cases = [(s, c) for s in range(2) for c in range(2)]
    axes = ("section", "core")
    same = jnp.where(core == 0, first, second)
    other = jnp.where(core == 0, second, first)
    same = lax.ppermute(same, axes, [(s * 2 + h, h * 2 + s) for s, h in cases])
    other = lax.ppermute(other, axes, [(s * 2 + h, (1 - h) * 2 + s) for s, h in cases])
    top = jnp.where(section == 0, same, other)
    bottom = jnp.where(section == 0, other, same)
    return jnp.concatenate([top, bottom], axis=0)


def normalize(values):
    center = values - jnp.mean(values, axis=-1, keepdims=True)
    spread = jnp.mean(center * center, axis=-1, keepdims=True)
    scale = lax.rsqrt(spread + NORM_EPS)
    return (center * scale, scale)


def modulate(values, shift, scale):
    return normalize(values)[0] * (1.0 + scale) + shift


def modulate_back(grad, values, scale):
    unit, inverse = normalize(values)
    shift_grad = jnp.sum(grad, axis=0)
    scale_grad = jnp.sum(grad * unit, axis=0)
    inner = grad * (1.0 + scale)
    mean_one = jnp.mean(inner, axis=-1, keepdims=True)
    mean_two = jnp.mean(inner * unit, axis=-1, keepdims=True)
    return ((inner - mean_one - unit * mean_two) * inverse, shift_grad, scale_grad)


def gelu_tanh(values):
    return jax.nn.gelu(values, approximate=True)


def time_embed(steps_in, model_width):
    half_width = model_width // 2
    frequency = jnp.exp(-math.log(10000.0) * jnp.arange(half_width, dtype=F32) / half_width)
    angles = steps_in.astype(F32)[:, None] * frequency[None, :]
    return jnp.concatenate([jnp.cos(angles), jnp.sin(angles)], axis=-1)


def split_heads(stacked):
    rows, width = stacked.shape
    parts = stacked.reshape(rows, 3, width // 3 // HEAD_DIM, HEAD_DIM)
    return parts[:, 0], parts[:, 1], parts[:, 2]


def scores_of(queries, keys_in, live):
    scores = jnp.einsum("qhe,khe->hqk", queries, keys_in, preferred_element_type=F32)
    return jnp.where(live[None, None, :] > 0, scores * HEAD_DIM ** (-0.5), MASK_SCORE)


def attend(stacked, live):
    queries, keys_in, values = split_heads(stacked)
    scores = scores_of(queries, keys_in, live)
    row_peak = jnp.max(scores, axis=-1, keepdims=True)
    exponent = jnp.exp(scores - row_peak)
    row_total = jnp.sum(exponent, axis=-1, keepdims=True)
    probability = (exponent / row_total).astype(BF)
    attended = jnp.einsum("hqk,khe->qhe", probability, values, preferred_element_type=F32)
    return attended.astype(BF).reshape(stacked.shape[0], -1), row_peak + jnp.log(row_total)


def attend_back(attended_grad, stacked, live, log_total):
    rows = stacked.shape[0]
    queries, keys_in, values = split_heads(stacked)
    grad = attended_grad.reshape(values.shape)
    soft = jnp.exp(scores_of(queries, keys_in, live) - log_total)
    value_grad = jnp.einsum("hqk,qhe->khe", soft.astype(BF), grad, preferred_element_type=F32)
    prob_grad = jnp.einsum("qhe,khe->hqk", grad, values, preferred_element_type=F32)
    score_grad = soft * (prob_grad - jnp.sum(soft * prob_grad, axis=-1, keepdims=True))
    score_grad = score_grad.astype(BF)
    scale = HEAD_DIM ** (-0.5)
    query_grad = jnp.einsum("hqk,khe->qhe", score_grad, keys_in, preferred_element_type=F32) * scale
    key_grad = jnp.einsum("hqk,qhe->khe", score_grad, queries, preferred_element_type=F32) * scale
    stacked_grad = jnp.stack([query_grad, key_grad, value_grad], axis=1).astype(BF)
    return stacked_grad.reshape(rows, -1)


def block_attention(inputs, mod, live, w_attn, own_count):
    columns = w_attn.shape[1] // 4
    shift_a, scale_a, gate_a, shift_b, scale_b = (mod[i][None] for i in range(5))
    normed = modulate(inputs, shift_a, scale_a).astype(BF)
    stacked = mm(normed, w_attn[:, : 3 * columns], BF)
    attended, log_total = attend(stacked, live)
    branch_a = sum_rows(mm_nt(attended, w_attn[:, 3 * columns :]))
    hidden = inputs[:own_count] + gate_a * branch_a
    normed_b = gather_rows(modulate(hidden, shift_b, scale_b).astype(BF))
    return (normed, stacked, attended, log_total, branch_a, hidden, normed_b)


def block_back_feed(grad_all, mod, saved, w_up, w_down, up_value, activated):
    hidden, normed_b, branch_b, branch_a = saved
    own_count = hidden.shape[0]
    gate_a, scale_b, gate_b = (mod[i][None] for i in (2, 4, 5))
    grad_own = grad_all[:own_count]
    gate_b_grad = jnp.sum(grad_own * branch_b, axis=0)
    down_in = (gate_b * grad_all).astype(BF)
    grad_down = mm_tn(down_in, activated, BF)
    act_grad = mm(down_in, w_down)
    up_grad = jax.vjp(gelu_tanh, up_value)[1](act_grad)[0].astype(BF)
    grad_up = mm_tn(normed_b, up_grad, BF)
    normed_grad = sum_rows(mm_nt(up_grad, w_up))
    hidden_grad, shift_b_grad, scale_b_grad = modulate_back(normed_grad, hidden, scale_b)
    hidden_grad = hidden_grad + grad_own
    gate_a_grad = jnp.sum(hidden_grad * branch_a, axis=0)
    output_in = gather_rows((gate_a * hidden_grad).astype(BF))
    return (
        hidden_grad,
        output_in,
        grad_up,
        grad_down,
        (gate_a_grad, shift_b_grad, scale_b_grad, gate_b_grad),
    )


def block_back_attention(output_in, hidden_grad, inputs_own, mod, live, saved, w_attn):
    normed, stacked, attended, log_total = saved
    columns = w_attn.shape[1] // 4
    grad_output = mm_tn(output_in, attended, BF)
    attended_grad = mm(output_in, w_attn[:, 3 * columns :], BF)
    stacked_grad = attend_back(attended_grad, stacked, live, log_total)
    grad_heads = mm_tn(normed, stacked_grad, BF)
    normed_grad = sum_rows(mm_nt(stacked_grad, w_attn[:, : 3 * columns]))
    input_grad, shift_a_grad, scale_a_grad = modulate_back(normed_grad, inputs_own, mod[1][None])
    grad_attn = jnp.concatenate([grad_heads, grad_output], axis=1)
    return (input_grad + hidden_grad, grad_attn, shift_a_grad, scale_a_grad)


def adam_update(weight_in, first_in, second_in, gradient, factor):
    clipped = gradient * factor
    first_out = BETA_ONE * first_in + (1.0 - BETA_ONE) * clipped
    second_out = BETA_TWO * second_in + (1.0 - BETA_TWO) * clipped * clipped
    ratio = (
        first_out
        / (1.0 - BETA_ONE**STEP)
        / (jnp.sqrt(second_out / (1.0 - BETA_TWO**STEP)) + ADAM_EPS)
    )
    weight_out = weight_in - LEARN_RATE * (ratio + WEIGHT_DECAY * weight_in)
    return (weight_out, first_out, second_out)


def per_device(
    tokens,
    cotangent,
    kept_index,
    full_flag,
    labels,
    timesteps,
    class_table,
    heads_weight,
    heads_first,
    heads_second,
    output_weight,
    output_first,
    output_second,
    up_weight,
    up_first,
    up_second,
    down_weight,
    down_first,
    down_second,
    adaln_weight,
    adaln_first,
    adaln_second,
    mask_token,
    mask_first,
    mask_second,
):
    image_count, seq_length, model_width = tokens.shape
    section = lax.axis_index("section")
    core = lax.axis_index("core")
    plane = lax.axis_index("dp")
    chip = lax.axis_index("row") * 2 + section
    quarter = seq_length // 4
    shard = model_width // lax.axis_size("dp")
    columns = heads_weight.shape[-1]

    with jax.named_scope("weights_in"):
        attn_pack = jnp.concatenate(
            [heads_weight[0, 0], heads_weight[0, 1], heads_weight[0, 2], output_weight[0].T], axis=1
        ).astype(BF)
        packs = (attn_pack, up_weight[0].astype(BF), down_weight[0].T.astype(BF))
        shares = [send_shares(pack, section) for pack in packs]
        enc_half = [jnp.where(core == 0, same, other) for same, other in shares]
        dec_half = [jnp.where(core == 0, other, same) for same, other in shares]

        def gather_weight(half):
            return lax.all_gather(half, ROWS_BY, axis=0, tiled=True)

        enc_w = [gather_weight(half) for half in enc_half]
        dec_w = [gather_weight(half) for half in dec_half]

    with jax.named_scope("modulation"):
        codes = planes_gather(jnp.stack([labels, timesteps], axis=1))
        class_count = class_table.shape[0]
        label_hot = (codes[:, :1] == jnp.arange(class_count, dtype=jnp.int32)[None, :]).astype(BF)
        condition = mm(label_hot, class_table) + time_embed(codes[:, 1], model_width)
        cond_act = jax.nn.silu(condition).astype(BF)
        cond_rows = lax.dynamic_slice_in_dim(cond_act, plane * shard, shard, 1)
        adaln_part = planes_sum(mm(cond_rows, adaln_weight[0].astype(BF)))
        adaln_all = lax.all_gather(adaln_part, PLANE, axis=0, tiled=False)
        mod_all = lax.dynamic_index_in_dim(adaln_all, core, 1, keepdims=False)
        mod_all = mod_all.reshape(2, 6, model_width)
        enc_mod, dec_mod = mod_all[0], mod_all[1]

    def relative(values):
        parts = [
            lax.dynamic_slice_in_dim(values, (chip ^ offset) * quarter, quarter, 0)
            for offset in range(4)
        ]
        return jnp.concatenate(parts, axis=0)

    with jax.named_scope("placement"):
        image_tokens = lax.dynamic_index_in_dim(tokens, core, 0, keepdims=False)
        image_cot = relative(lax.dynamic_index_in_dim(cotangent, core, 0, keepdims=False))
        kept = relative(lax.dynamic_index_in_dim(kept_index, core, 0, keepdims=False))
        flag = lax.dynamic_index_in_dim(full_flag, core, 0, keepdims=False)
        plain_ids = jnp.arange(seq_length, dtype=jnp.int32)
        ids = ((plain_ids // quarter) ^ chip) * quarter + plain_ids % quarter
        live = ids < jnp.where(flag > 0, seq_length, seq_length // 2)
        place_plain = ((kept[:, None] == plain_ids[None, :]) & live[:, None]).astype(BF)
        place = ((kept[:, None] == ids[None, :]) & live[:, None]).astype(BF)
        live = live.astype(F32)
        uncovered = 1.0 - jnp.sum(place.astype(F32), axis=0)
        restore = (ids[:, None] == plain_ids[None, :]).astype(BF)
        enc_in = mm(place_plain, image_tokens)

    with jax.named_scope("encoder"):
        normed, stacked, attended, log_total, branch_a, hidden, normed_b = block_attention(
            enc_in, enc_mod, live, enc_w[0], quarter
        )
        up_value = mm(normed_b, enc_w[1])
        activated = gelu_tanh(up_value).astype(BF)
        branch_b = sum_rows(mm_nt(activated, enc_w[2]))
        enc_out = (hidden + enc_mod[5][None] * branch_b) * live[:quarter, None]
        sent = gather_rows(enc_out.astype(BF))
        enc_attn_saved = (normed, stacked, attended, log_total)
        enc_feed_saved = (hidden, normed_b, branch_b, branch_a)
        enc_up, enc_act = up_value, activated

    with jax.named_scope("decoder"):
        dec_in = mm_tn(place, sent) + uncovered[:, None] * mask_token[None, :]
        all_live = jnp.ones_like(live)
        normed, stacked, attended, log_total, branch_a, hidden, normed_b = block_attention(
            dec_in, dec_mod, all_live, dec_w[0], quarter
        )
        up_value = mm(normed_b, dec_w[1])
        activated = gelu_tanh(up_value).astype(BF)
        branch_b = sum_rows(mm_nt(activated, dec_w[2]))
        dec_out = gather_rows((hidden + dec_mod[5][None] * branch_b).astype(BF))
        dec_attn_saved = (normed, stacked, attended, log_total)
        dec_feed_saved = (hidden, normed_b, branch_b, branch_a)

    def reduce_grad(grad):
        return lax.psum_scatter(grad, ROWS_BY, scatter_dimension=0, tiled=True)

    with jax.named_scope("decoder_back"):
        hidden_grad, output_in, grad_up, grad_down, mods = block_back_feed(
            image_cot.astype(F32), dec_mod, dec_feed_saved, dec_w[1], dec_w[2], up_value, activated
        )
        dec_sums = [None, reduce_grad(grad_up), reduce_grad(grad_down)]
        dec_grad, grad_attn, shift_grad, scale_grad = block_back_attention(
            output_in, hidden_grad, dec_in[:quarter], dec_mod, all_live, dec_attn_saved, dec_w[0]
        )
        dec_sums[0] = reduce_grad(grad_attn)
        dec_mods = (shift_grad, scale_grad) + mods
        mask_part = jnp.sum(uncovered[:quarter, None] * dec_grad, axis=0)
        dec_low = gather_rows(dec_grad.astype(BF))

    with jax.named_scope("encoder_back"):
        enc_cot = mm(place, dec_low)
        hidden_grad, output_in, grad_up, grad_down, mods = block_back_feed(
            enc_cot, enc_mod, enc_feed_saved, enc_w[1], enc_w[2], enc_up, enc_act
        )
        enc_sums = [None, reduce_grad(grad_up), reduce_grad(grad_down)]
        enc_grad, grad_attn, shift_grad, scale_grad = block_back_attention(
            output_in, hidden_grad, enc_in[:quarter], enc_mod, live, enc_attn_saved, enc_w[0]
        )
        enc_sums[0] = reduce_grad(grad_attn)
        enc_mods = (shift_grad, scale_grad) + mods
        enc_low = gather_rows(enc_grad.astype(BF))

    with jax.named_scope("modulation_back"):
        mod_parts = jnp.stack([jnp.concatenate(enc_mods), jnp.concatenate(dec_mods)])
        mod_parts = mod_parts.reshape(8, -1)
        mod_parts = lax.all_to_all(mod_parts, PLANE, 0, 0, tiled=True)
        mod_grad = jnp.sum(mod_parts.reshape(4, 2, -1), axis=0)
        mod_grad = planes_gather(mod_grad)
        grad_adaln = lax.dot_general(
            cond_rows.astype(F32), mod_grad, (((0,), (0,)), ((), ())), precision=PRECISE
        )

    with jax.named_scope("norm"):
        square = jnp.sum(grad_adaln * grad_adaln)
        for part in enc_sums + dec_sums:
            wide = part.astype(F32)
            square = square + jnp.sum(wide * wide)
        totals = jnp.concatenate([mask_part, jnp.full((128,), square / 128.0, F32)])
        totals = sum_everywhere(totals.reshape(1, -1))[0]
        mask_total = totals[:model_width]
        grad_norm = jnp.sqrt(jnp.sum(totals[model_width:]) + jnp.sum(mask_total * mask_total))
        factor = jnp.minimum(1.0, CLIP_NORM / (grad_norm + NORM_EPS))

    with jax.named_scope("update"):
        own = [
            return_shares(first, second, section, core).astype(F32)
            for first, second in zip(enc_sums, dec_sums)
        ]
        heads_grad = own[0][:, : 3 * columns].reshape(shard, 3, columns).transpose(1, 0, 2)
        gradients = (
            heads_grad[None],
            own[0][:, 3 * columns :].T[None],
            own[1][None],
            own[2].T[None],
            grad_adaln[None],
        )
        masters = (heads_weight, output_weight, up_weight, down_weight, adaln_weight)
        firsts = (heads_first, output_first, up_first, down_first, adaln_first)
        seconds = (heads_second, output_second, up_second, down_second, adaln_second)
        updated = []
        for position in range(5):
            updated += adam_update(
                masters[position], firsts[position], seconds[position], gradients[position], factor
            )
        mask_next = adam_update(mask_token, mask_first, mask_second, mask_total, factor)

    with jax.named_scope("outputs"):

        def both_images(mine):
            other = swap_cores(mine)
            pair = jnp.where(core == 0, jnp.stack([mine, other]), jnp.stack([other, mine]))
            return pair[None]

        is_first = section == 0
        layer_out = mm_tn(restore, jnp.where(is_first, sent, dec_out), BF)
        arrange = jnp.where(is_first, place_plain, restore)
        in_grads = mm_tn(arrange, jnp.where(is_first, enc_low, dec_low), BF)
        layer_out, in_grads = both_images(layer_out), both_images(in_grads)

    return (layer_out, in_grads, *updated, *mask_next, grad_norm)


def solution(mesh):
    sizes = dict(mesh.shape)
    parted = Mesh(
        mesh.devices.reshape(sizes["section"], sizes["tensor"] // 2, 2, sizes["dp"]),
        ("section", "row", "core", "dp"),
    )
    tensor = ("row", "core")
    heads = P("section", None, "dp", tensor)
    tensor_dp = P("section", tensor, "dp")
    dp_tensor = P("section", "dp", tensor)
    weights = [heads] * 3 + [tensor_dp] * 3 + [dp_tensor] * 3 + [tensor_dp] * 3 + [dp_tensor] * 3
    images = P("dp", None, None)
    layers = P("section", "dp", None, None)
    return jax.shard_map(
        per_device,
        mesh=parted,
        in_specs=(
            images,
            images,
            P("dp", None),
            P("dp"),
            P("dp"),
            P("dp"),
            P(),
            *weights,
            P(),
            P(),
            P(),
        ),
        out_specs=(layers, layers, *weights, P(), P(), P(), P()),
        check_vma=False,
    )
```

```python
import math

import jax
import jax.numpy as jnp
from jax import lax
from jax.sharding import Mesh
from jax.sharding import PartitionSpec as P

HEAD_DIM = 72
STEP = 10

PRECISE = lax.Precision.HIGHEST
NORM_EPS = 1e-06
BETA_ONE = 0.9
BETA_TWO = 0.99
LEARN_RATE = 0.05
WEIGHT_DECAY = 0.01
ADAM_EPS = 1e-08
CLIP_NORM = 1.0
MASK_SCORE = -1000000000.0

BF = jnp.bfloat16
F32 = jnp.float32
PLANE = ("section", "row", "core")
CHIPS = ("section", "row")
ROWS_BY = ("dp", "core")


def dot(left, right, dims, out=F32):
    return lax.dot_general(left, right, (dims, ((), ())), preferred_element_type=F32).astype(out)


def mm(left, right, out=F32):
    return dot(left, right, ((1,), (0,)), out)


def mm_nt(left, right, out=F32):
    return dot(left, right, ((1,), (1,)), out)


def mm_tn(left, right, out=F32):
    return dot(left, right, ((0,), (0,)), out)


def turned(values):
    return mm_tn(values, jnp.eye(values.shape[0], dtype=values.dtype), values.dtype)


def paired(left_one, right_one, left_two, right_two):
    one, two = right_one.shape[1], right_two.shape[1]
    lefts = jnp.concatenate([left_one, left_two], axis=0)
    rights = jnp.concatenate(
        [jnp.pad(right_one, ((0, 0), (0, two))), jnp.pad(right_two, ((0, 0), (one, 0)))], axis=0
    )
    return mm_tn(lefts, rights, BF)


def chip_route(offset):
    return [
        (s * 2 + r, (s ^ (offset & 1)) * 2 + (r ^ (offset >> 1)))
        for s in range(2)
        for r in range(2)
    ]


def swap_chips(block, offset):
    return lax.ppermute(block, CHIPS, chip_route(offset))


def swap_cores(block):
    return lax.ppermute(block, "core", [(0, 1), (1, 0)])


def gather_rows(own):
    return jnp.concatenate([own] + [swap_chips(own, offset) for offset in (1, 2, 3)], axis=0)


def sum_rows(partial):
    count = partial.shape[0] // 4
    low = partial.astype(BF)
    total = partial[:count]
    for offset in (1, 2, 3):
        total = total + swap_chips(low[offset * count : (offset + 1) * count], offset).astype(F32)
    return total


def xor_route(size, offset):
    return [(i, i ^ offset) for i in range(size)]


def planes_gather(block):
    size = lax.axis_size("dp")
    parts = [block] + [
        lax.ppermute(block, "dp", xor_route(size, offset)) for offset in range(1, size)
    ]
    return jnp.concatenate(parts, axis=0)


def planes_sum(blocks):
    size = lax.axis_size("dp")
    count = blocks.shape[0] // size
    total = blocks[:count]
    for offset in range(1, size):
        part = blocks[offset * count : (offset + 1) * count]
        total = total + lax.ppermute(part, "dp", xor_route(size, offset))
    return total


def sum_everywhere(values):
    for axis in ("dp", "row", "section", "core"):
        size = lax.axis_size(axis)
        step = 1
        while step < size:
            values = values + lax.ppermute(values, axis, xor_route(size, step))
            step *= 2
    return values


def send_shares(pack, section, core, later=None):
    half = pack.shape[0] // 2
    mine = lax.dynamic_slice_in_dim(pack, core * half, half, 0)
    other = swap_cores(lax.dynamic_slice_in_dim(pack, (1 - core) * half, half, 0))
    keep = jnp.where(core == section, mine, other)
    give = jnp.where(core == section, other, mine)
    if later is not None:
        give, later = tie(give, later)
    given = lax.ppermute(give, "section", [(0, 1), (1, 0)])
    return (jnp.where(section == 0, keep, given), jnp.where(section == 0, given, keep), later)


def return_shares(first, second, section, core):
    keep = jnp.where(section == 0, first, second)
    give = jnp.where(section == 0, second, first)
    given = lax.ppermute(give, "section", [(0, 1), (1, 0)])
    mine = jnp.where(core == section, keep, given)
    other = swap_cores(jnp.where(core == section, given, keep))
    top = jnp.where(core == 0, mine, other)
    bottom = jnp.where(core == 0, other, mine)
    return jnp.concatenate([top, bottom], axis=0)


def tie(*values):
    return lax.optimization_barrier(values)


def gather_weight(half):
    return lax.all_gather(half, ROWS_BY, axis=0, tiled=True)


def sum_cores(core, *grads):
    planes = lax.axis_size("dp")
    sums = []
    for grad in grads:
        halves = grad.reshape(planes, 2, grad.shape[0] // planes // 2, grad.shape[1])
        theirs = swap_cores(lax.dynamic_index_in_dim(halves, 1 - core, 1, keepdims=False))
        mine = lax.dynamic_index_in_dim(halves, core, 1, keepdims=False)
        sums.append((mine.astype(F32) + theirs.astype(F32)).astype(BF))
    return jnp.concatenate(sums, axis=2)


def sum_planes(grad):
    summed = lax.psum_scatter(grad, "dp", scatter_dimension=0, tiled=True)
    return summed.reshape(summed.shape[1:])


def normalize(values):
    center = values - jnp.mean(values, axis=-1, keepdims=True)
    spread = jnp.mean(center * center, axis=-1, keepdims=True)
    scale = lax.rsqrt(spread + NORM_EPS)
    return (center * scale, scale)


def modulate(values, shift, scale):
    return normalize(values)[0] * (1.0 + scale) + shift


def modulate_back(grad, values, scale):
    unit, inverse = normalize(values)
    shift_grad = jnp.sum(grad, axis=0)
    scale_grad = jnp.sum(grad * unit, axis=0)
    inner = grad * (1.0 + scale)
    mean_one = jnp.mean(inner, axis=-1, keepdims=True)
    mean_two = jnp.mean(inner * unit, axis=-1, keepdims=True)
    return ((inner - mean_one - unit * mean_two) * inverse, shift_grad, scale_grad)


def gelu_tanh(values):
    return jax.nn.gelu(values, approximate=True)


def time_embed(steps_in, model_width):
    half_width = model_width // 2
    frequency = jnp.exp(-math.log(10000.0) * jnp.arange(half_width, dtype=F32) / half_width)
    angles = steps_in.astype(F32)[:, None] * frequency[None, :]
    return jnp.concatenate([jnp.cos(angles), jnp.sin(angles)], axis=-1)


def split_heads(stacked):
    rows, width = stacked.shape
    parts = stacked.reshape(rows, 3, width // 3 // HEAD_DIM, HEAD_DIM)
    return parts[:, 0], parts[:, 1], parts[:, 2]


def scores_of(queries, keys_in, live):
    scores = jnp.einsum("qhe,khe->hqk", queries, keys_in, preferred_element_type=F32)
    return jnp.where(live[None, None, :] > 0, scores * HEAD_DIM ** (-0.5), MASK_SCORE)


def attend(stacked, live):
    queries, keys_in, values = split_heads(stacked)
    scores = scores_of(queries, keys_in, live)
    row_peak = jnp.max(scores, axis=-1, keepdims=True)
    exponent = jnp.exp(scores - row_peak)
    row_total = jnp.sum(exponent, axis=-1, keepdims=True)
    probability = (exponent / row_total).astype(BF)
    attended = jnp.einsum("hqk,khe->qhe", probability, values, preferred_element_type=F32)
    return attended.astype(BF).reshape(stacked.shape[0], -1), row_peak + jnp.log(row_total)


def attend_back(attended_grad, stacked, live, log_total):
    rows = stacked.shape[0]
    queries, keys_in, values = split_heads(stacked)
    grad = attended_grad.reshape(values.shape)
    soft = jnp.exp(scores_of(queries, keys_in, live) - log_total)
    value_grad = jnp.einsum("hqk,qhe->khe", soft.astype(BF), grad, preferred_element_type=F32)
    prob_grad = jnp.einsum("qhe,khe->hqk", grad, values, preferred_element_type=F32)
    score_grad = soft * (prob_grad - jnp.sum(soft * prob_grad, axis=-1, keepdims=True))
    score_grad = score_grad.astype(BF)
    scale = HEAD_DIM ** (-0.5)
    query_grad = jnp.einsum("hqk,khe->qhe", score_grad, keys_in, preferred_element_type=F32) * scale
    key_grad = jnp.einsum("hqk,qhe->khe", score_grad, queries, preferred_element_type=F32) * scale
    stacked_grad = jnp.stack([query_grad, key_grad, value_grad], axis=1).astype(BF)
    return stacked_grad.reshape(rows, -1)


def block_attention(inputs, mod, live, w_attn, own_count):
    columns = w_attn.shape[1] // 4
    shift_a, scale_a, gate_a, shift_b, scale_b = (mod[i][None] for i in range(5))
    normed = modulate(inputs, shift_a, scale_a).astype(BF)
    stacked = mm(normed, w_attn[:, : 3 * columns], BF)
    attended, log_total = attend(stacked, live)
    branch_a = sum_rows(mm_nt(attended, w_attn[:, 3 * columns :]))
    hidden = inputs[:own_count] + gate_a * branch_a
    normed_b = gather_rows(modulate(hidden, shift_b, scale_b).astype(BF))
    return (normed, stacked, attended, log_total, branch_a, hidden, normed_b)


def block_back_feed(grad_all, mod, saved, w_up, w_down, up_value, activated, split, core, earlier):
    hidden, normed_b, branch_a = saved
    own_count = hidden.shape[0]
    gate_a, scale_b, gate_b = (mod[i][None] for i in (2, 4, 5))
    grad_own = grad_all[:own_count]
    down_in = (gate_b * grad_all).astype(BF)
    if split:
        grad_down = mm_tn(down_in, activated, BF)
        down_in, grad_down = tie(down_in, grad_down)
        grad_down = sum_cores(core, grad_down)
    act_grad = mm(down_in, w_down)
    up_grad = jax.vjp(gelu_tanh, up_value)[1](act_grad)[0].astype(BF)
    sums = []
    if split:
        up_grad, grad_down = tie(up_grad, grad_down)
        sums.append(sum_planes(grad_down))
        earlier = sums
    partial, up_grad, down_in = tie(mm_nt(up_grad, w_up), up_grad, down_in)
    grads = [mm_tn(normed_b, up_grad, BF)]
    if not split:
        grads.append(mm_tn(down_in, activated, BF))
    normed_grad, grad_up = tie(sum_rows(partial), sum_cores(core, *grads))
    up_sum = sum_planes(grad_up)
    normed_grad, *earlier = tie(normed_grad, *earlier)
    hidden_grad, shift_b_grad, scale_b_grad = modulate_back(normed_grad, hidden, scale_b)
    hidden_grad = hidden_grad + grad_own
    gate_a_grad = jnp.sum(hidden_grad * branch_a, axis=0)
    output_in = gather_rows((gate_a * hidden_grad).astype(BF))
    mods = (gate_a_grad, shift_b_grad, scale_b_grad)
    return (hidden_grad, output_in, up_sum, mods, earlier)


def block_back_attention(output_in, hidden_grad, inputs_own, mod, live, saved, w_attn, core, earlier):
    normed, stacked, attended, log_total = saved
    columns = w_attn.shape[1] // 4
    attended_grad = mm(output_in, w_attn[:, 3 * columns :], BF)
    stacked_grad = attend_back(attended_grad, stacked, live, log_total)
    partial = mm_nt(stacked_grad, w_attn[:, : 3 * columns])
    partial, stacked_grad, output_in = tie(partial, stacked_grad, output_in)
    grad_attn = paired(normed, stacked_grad, output_in, attended)
    normed_grad, grad_attn = tie(sum_rows(partial), sum_cores(core, grad_attn))
    attn_sum = sum_planes(grad_attn)
    normed_grad, *earlier = tie(normed_grad, *earlier)
    input_grad, shift_a_grad, scale_a_grad = modulate_back(normed_grad, inputs_own, mod[1][None])
    input_grad = input_grad + hidden_grad
    low_grad = gather_rows(input_grad.astype(BF))
    return (input_grad, low_grad, attn_sum, shift_a_grad, scale_a_grad, earlier)


def squared(values):
    wide = values.astype(F32)
    return jnp.sum(wide * wide)


def adam_update(weight_in, first_in, second_in, gradient, factor):
    clipped = gradient * factor
    first_out = BETA_ONE * first_in + (1.0 - BETA_ONE) * clipped
    second_out = BETA_TWO * second_in + (1.0 - BETA_TWO) * clipped * clipped
    ratio = (
        first_out
        / (1.0 - BETA_ONE**STEP)
        / (jnp.sqrt(second_out / (1.0 - BETA_TWO**STEP)) + ADAM_EPS)
    )
    weight_out = weight_in - LEARN_RATE * (ratio + WEIGHT_DECAY * weight_in)
    return (weight_out, first_out, second_out)


def per_device(
    tokens,
    cotangent,
    kept_index,
    full_flag,
    labels,
    timesteps,
    class_table,
    heads_weight,
    heads_first,
    heads_second,
    output_weight,
    output_first,
    output_second,
    up_weight,
    up_first,
    up_second,
    down_weight,
    down_first,
    down_second,
    adaln_weight,
    adaln_first,
    adaln_second,
    mask_token,
    mask_first,
    mask_second,
):
    image_count, seq_length, model_width = tokens.shape
    section = lax.axis_index("section")
    core = lax.axis_index("core")
    plane = lax.axis_index("dp")
    chip = lax.axis_index("row") * 2 + section
    quarter = seq_length // 4
    shard = model_width // lax.axis_size("dp")
    columns = heads_weight.shape[-1]

    with jax.named_scope("weights_in"):
        attn_pack = jnp.concatenate(
            [heads_weight[0, 0], heads_weight[0, 1], heads_weight[0, 2], output_weight[0].T], axis=1
        ).astype(BF)
        *halves, feed_parts = send_shares(attn_pack, section, core, (up_weight[0], down_weight[0]))
        attn_half = jnp.concatenate(halves, axis=1)
        feed_pack = jnp.concatenate([feed_parts[0], feed_parts[1].T], axis=1).astype(BF)
        feed_pack, attn_half = tie(feed_pack, attn_half)
        attn_all = gather_weight(attn_half)
        attn_width = attn_pack.shape[1]
        enc_attn, dec_attn = attn_all[:, :attn_width], attn_all[:, attn_width:]
        enc_feed_half, dec_feed_half, _ = send_shares(feed_pack, section, core)
        feed_width = feed_pack.shape[1] // 2
        enc_feed = gather_weight(enc_feed_half)

    with jax.named_scope("modulation"):
        codes = planes_gather(jnp.stack([labels, timesteps], axis=1))
        class_count = class_table.shape[0]
        label_hot = (codes[:, :1] == jnp.arange(class_count, dtype=jnp.int32)[None, :]).astype(BF)
        condition = mm(label_hot, class_table) + time_embed(codes[:, 1], model_width)
        cond_act = jax.nn.silu(condition).astype(BF)
        cond_rows = lax.dynamic_slice_in_dim(cond_act, plane * shard, shard, 1)
        adaln_part = planes_sum(mm(cond_rows, adaln_weight[0].astype(BF)))
        adaln_all = lax.all_gather(adaln_part, PLANE, axis=0, tiled=False)
        mod_all = lax.dynamic_index_in_dim(adaln_all, core, 1, keepdims=False)
        mod_all = mod_all.reshape(2, 6, model_width)
        enc_mod, dec_mod = mod_all[0], mod_all[1]

    def relative(values):
        parts = [
            lax.dynamic_slice_in_dim(values, (chip ^ offset) * quarter, quarter, 0)
            for offset in range(4)
        ]
        return jnp.concatenate(parts, axis=0)

    with jax.named_scope("placement"):
        image_tokens = lax.dynamic_index_in_dim(tokens, core, 0, keepdims=False)
        image_cot = relative(lax.dynamic_index_in_dim(cotangent, core, 0, keepdims=False))
        kept = relative(lax.dynamic_index_in_dim(kept_index, core, 0, keepdims=False))
        flag = lax.dynamic_index_in_dim(full_flag, core, 0, keepdims=False)
        plain_ids = jnp.arange(seq_length, dtype=jnp.int32)
        ids = ((plain_ids // quarter) ^ chip) * quarter + plain_ids % quarter
        live = ids < jnp.where(flag > 0, seq_length, seq_length // 2)
        place_plain = ((kept[:, None] == plain_ids[None, :]) & live[:, None]).astype(BF)
        place = ((kept[:, None] == ids[None, :]) & live[:, None]).astype(BF)
        live = live.astype(F32)
        uncovered = 1.0 - jnp.sum(place.astype(F32), axis=0)
        restore = (ids[:, None] == plain_ids[None, :]).astype(BF)
        enc_in = mm(place_plain, image_tokens)

    def feed_up(normed_b, feed):
        up_value = mm(normed_b, feed[:, :feed_width])
        return up_value, gelu_tanh(up_value).astype(BF)

    def feed_down(activated, feed):
        return sum_rows(mm_nt(activated, feed[:, feed_width:]))

    with jax.named_scope("encoder"):
        normed, stacked, attended, log_total, branch_a, hidden, normed_b = block_attention(
            enc_in, enc_mod, live, enc_attn, quarter
        )
        normed_b, dec_feed_half = tie(normed_b, dec_feed_half)
        dec_feed = gather_weight(dec_feed_half)
        enc_up_value, enc_act = feed_up(normed_b, enc_feed)
        branch_b = feed_down(enc_act, enc_feed)
        enc_branch_b = branch_b
        enc_out = (hidden + enc_mod[5][None] * branch_b) * live[:quarter, None]
        sent = gather_rows(enc_out.astype(BF))
        enc_attn_saved = (normed, stacked, attended, log_total)
        enc_feed_saved = (hidden, normed_b, branch_a)

    with jax.named_scope("decoder"):
        dec_in = mm_tn(place, sent) + uncovered[:, None] * mask_token[None, :]
        all_live = jnp.ones_like(live)
        normed, stacked, attended, log_total, branch_a, hidden, normed_b = block_attention(
            dec_in, dec_mod, all_live, dec_attn, quarter
        )
        dec_up_value, dec_act = feed_up(normed_b, dec_feed)
        dec_attn_saved = (normed, stacked, attended, log_total)
        dec_feed_saved = (hidden, normed_b, branch_a)

    with jax.named_scope("decoder_back"):
        hidden_grad, output_in, dec_up_sum, mods, (dec_down_sum,) = block_back_feed(
            image_cot.astype(F32),
            dec_mod,
            dec_feed_saved,
            dec_feed[:, :feed_width],
            dec_feed[:, feed_width:],
            dec_up_value,
            dec_act,
            True,
            core,
            [],
        )
        dec_grad, dec_low, dec_attn_sum, shift_grad, scale_grad, _ = block_back_attention(
            output_in,
            hidden_grad,
            dec_in[:quarter],
            dec_mod,
            all_live,
            dec_attn_saved,
            dec_attn,
            core,
            [],
        )
        dec_low, dec_up_sum, dec_act = tie(dec_low, dec_up_sum, dec_act)
        branch_b = feed_down(dec_act, dec_feed)
        dec_out = dec_feed_saved[0] + dec_mod[5][None] * branch_b
        gate_grad = jnp.sum(image_cot[:quarter].astype(F32) * branch_b, axis=0)
        dec_mods = (shift_grad, scale_grad) + mods + (gate_grad,)
        mask_part = jnp.sum(uncovered[:quarter, None] * dec_grad, axis=0)

    is_first = section == 0

    def both_images(mine):
        other = swap_cores(mine)
        pair = jnp.where(core == 0, jnp.stack([mine, other]), jnp.stack([other, mine]))
        return pair[None]

    with jax.named_scope("encoder_back"):
        enc_cot = mm(place, dec_low)
        enc_gate_grad = jnp.sum(enc_cot[:quarter] * enc_branch_b, axis=0)
        hidden_grad, output_in, enc_feed_sum, mods, (dec_attn_sum,) = block_back_feed(
            enc_cot,
            enc_mod,
            enc_feed_saved,
            enc_feed[:, :feed_width],
            enc_feed[:, feed_width:],
            enc_up_value,
            enc_act,
            False,
            core,
            [dec_attn_sum],
        )
        output_in, dec_out = tie(output_in, dec_out.astype(BF))
        dec_out = gather_rows(dec_out)
        layer_out = both_images(mm_tn(restore, jnp.where(is_first, sent, dec_out), BF))
        enc_grad, enc_low, enc_attn_sum, shift_grad, scale_grad, (enc_feed_sum, layer_out) = block_back_attention(
            output_in,
            hidden_grad,
            enc_in[:quarter],
            enc_mod,
            live,
            enc_attn_saved,
            enc_attn,
            core,
            [enc_feed_sum, layer_out],
        )
        enc_mods = (shift_grad, scale_grad) + mods + (enc_gate_grad,)

    with jax.named_scope("modulation_back"):
        mod_parts = jnp.stack([jnp.concatenate(enc_mods), jnp.concatenate(dec_mods)])
        mod_parts = lax.all_to_all(mod_parts.reshape(8, -1), PLANE, 0, 0, tiled=True)
        mod_parts, enc_feed_sum = tie(mod_parts, enc_feed_sum)
        mod_grad = planes_gather(jnp.sum(mod_parts.reshape(4, 2, -1), axis=0))

    with jax.named_scope("outputs"):
        arrange = jnp.where(is_first, place_plain, restore)
        in_grads = both_images(mm_tn(arrange, jnp.where(is_first, enc_low, dec_low), BF))

    with jax.named_scope("returns"):
        dec_feed_sum = jnp.concatenate([dec_up_sum, dec_down_sum], axis=1)
        feed_grad = return_shares(enc_feed_sum, dec_feed_sum, section, core)
        down_grad = turned(feed_grad[:, feed_width:])
        up_grad = feed_grad[:, :feed_width]

    with jax.named_scope("modulation_back"):
        grad_adaln = lax.dot_general(
            cond_rows.astype(F32), mod_grad, (((0,), (0,)), ((), ())), precision=PRECISE
        )

    with jax.named_scope("norm"):
        square = jnp.sum(grad_adaln * grad_adaln)
        for part in (dec_attn_sum, up_grad, down_grad):
            square = square + squared(part)
        square, grad_adaln, up_grad, down_grad, dec_attn_sum, enc_attn_sum = tie(
            square, grad_adaln, up_grad, down_grad, dec_attn_sum, enc_attn_sum
        )
        square = square + squared(enc_attn_sum)
        totals = jnp.concatenate([mask_part, jnp.full((128,), square / 128.0, F32)])
        totals = sum_everywhere(totals.reshape(1, -1))[0]
        attn_grad = return_shares(enc_attn_sum, dec_attn_sum, section, core)
        heads_grad = jnp.stack([attn_grad[:, i * columns : (i + 1) * columns] for i in range(3)])
        output_grad = turned(attn_grad[:, 3 * columns :])
        totals, heads_grad, output_grad = tie(totals, heads_grad, output_grad)
        mask_total = totals[:model_width]
        grad_norm = jnp.sqrt(jnp.sum(totals[model_width:]) + jnp.sum(mask_total * mask_total))
        factor = jnp.minimum(1.0, CLIP_NORM / (grad_norm + NORM_EPS))

    with jax.named_scope("update"):
        gradients = [
            part.astype(F32)[None] for part in (heads_grad, output_grad, up_grad, down_grad)
        ] + [grad_adaln[None]]
        masters = (heads_weight, output_weight, up_weight, down_weight, adaln_weight)
        firsts = (heads_first, output_first, up_first, down_first, adaln_first)
        seconds = (heads_second, output_second, up_second, down_second, adaln_second)
        updated = []
        for position in range(5):
            updated += adam_update(
                masters[position], firsts[position], seconds[position], gradients[position], factor
            )
        mask_next = adam_update(mask_token, mask_first, mask_second, mask_total, factor)

    return (layer_out, in_grads, *updated, *mask_next, grad_norm)


def solution(mesh):
    sizes = dict(mesh.shape)
    parted = Mesh(
        mesh.devices.reshape(sizes["section"], sizes["tensor"] // 2, 2, sizes["dp"]),
        ("section", "row", "core", "dp"),
    )
    tensor = ("row", "core")
    heads = P("section", None, "dp", tensor)
    tensor_dp = P("section", tensor, "dp")
    dp_tensor = P("section", "dp", tensor)
    weights = [heads] * 3 + [tensor_dp] * 3 + [dp_tensor] * 3 + [tensor_dp] * 3 + [dp_tensor] * 3
    images = P("dp", None, None)
    layers = P("section", "dp", None, None)
    return jax.shard_map(
        per_device,
        mesh=parted,
        in_specs=(
            images,
            images,
            P("dp", None),
            P("dp"),
            P("dp"),
            P("dp"),
            P(),
            *weights,
            P(),
            P(),
            P(),
        ),
        out_specs=(layers, layers, *weights, P(), P(), P(), P()),
        check_vma=False,
    )
```

```python
import math

import jax
import jax.numpy as jnp
from jax import lax
from jax.experimental import pallas as pl
from jax.experimental.pallas import tpu as pltpu
from jax.sharding import Mesh
from jax.sharding import PartitionSpec as P

HEAD_DIM = 72
STEP = 10

PRECISE = lax.Precision.HIGHEST
NORM_EPS = 1e-06
BETA_ONE = 0.9
BETA_TWO = 0.99
LEARN_RATE = 0.05
WEIGHT_DECAY = 0.01
ADAM_EPS = 1e-08
CLIP_NORM = 1.0
MASK_SCORE = -1000000000.0

BF = jnp.bfloat16
F32 = jnp.float32
PLANE = ("section", "row", "core")
CHIPS = ("section", "row")
ROWS_BY = ("dp", "core")


def dot(left, right, dims, out=F32):
    return lax.dot_general(left, right, (dims, ((), ())), preferred_element_type=F32).astype(out)


def mm(left, right, out=F32):
    return dot(left, right, ((1,), (0,)), out)


def mm_nt(left, right, out=F32):
    return dot(left, right, ((1,), (1,)), out)


def mm_tn(left, right, out=F32):
    return dot(left, right, ((0,), (0,)), out)


def turned(values):
    return mm_tn(values, jnp.eye(values.shape[0], dtype=values.dtype), values.dtype)


def chip_route(offset):
    return [
        (s * 2 + r, (s ^ (offset & 1)) * 2 + (r ^ (offset >> 1)))
        for s in range(2)
        for r in range(2)
    ]


def swap_chips(block, offset):
    return lax.ppermute(block, CHIPS, chip_route(offset))


def swap_cores(block):
    return lax.ppermute(block, "core", [(0, 1), (1, 0)])


def gather_rows(own):
    return jnp.concatenate([own] + [swap_chips(own, offset) for offset in (1, 2, 3)], axis=0)


def spread_rows(partial):
    count = partial.shape[0] // 4
    parts = [
        swap_chips(partial[offset * count : (offset + 1) * count], offset) for offset in (3, 2, 1)
    ]
    return [partial[:count]] + parts


def sum_rows(partial):
    return sum(part.astype(F32) for part in spread_rows(partial))


def xor_route(size, offset):
    return [(i, i ^ offset) for i in range(size)]


def planes_gather(block):
    size = lax.axis_size("dp")
    parts = [block] + [
        lax.ppermute(block, "dp", xor_route(size, offset)) for offset in range(1, size)
    ]
    return jnp.concatenate(parts, axis=0)


def planes_sum(blocks):
    size = lax.axis_size("dp")
    count = blocks.shape[0] // size
    total = blocks[:count]
    for offset in range(1, size):
        part = blocks[offset * count : (offset + 1) * count]
        total = total + lax.ppermute(part, "dp", xor_route(size, offset))
    return total


def sum_over(values, axes):
    for axis in axes:
        size = lax.axis_size(axis)
        step = 1
        while step < size:
            values = values + lax.ppermute(values, axis, xor_route(size, step))
            step *= 2
    return values


def send_shares(pack, section, core, later=None):
    half = pack.shape[0] // 2
    mine = lax.dynamic_slice_in_dim(pack, core * half, half, 0)
    other = swap_cores(lax.dynamic_slice_in_dim(pack, (1 - core) * half, half, 0))
    keep = jnp.where(core == section, mine, other)
    give = jnp.where(core == section, other, mine)
    if later is not None:
        give, later = tie(give, later)
    given = lax.ppermute(give, "section", [(0, 1), (1, 0)])
    return (jnp.where(section == 0, keep, given), jnp.where(section == 0, given, keep), later)


def return_over_section(first, second, section):
    keep = jnp.where(section == 0, first, second)
    give = jnp.where(section == 0, second, first)
    return (keep, lax.ppermute(give, "section", [(0, 1), (1, 0)]))


def return_over_core(keep, given, section, core):
    mine = jnp.where(core == section, keep, given)
    other = swap_cores(jnp.where(core == section, given, keep))
    top = jnp.where(core == 0, mine, other)
    bottom = jnp.where(core == 0, other, mine)
    return jnp.concatenate([top, bottom], axis=0)


def tie(*values):
    return lax.optimization_barrier(values)


def gather_weight(half):
    return lax.all_gather(half, ROWS_BY, axis=0, tiled=True)


def sum_cores(core, *grads):
    planes = lax.axis_size("dp")
    sums = []
    for grad in grads:
        halves = grad.reshape(planes, 2, grad.shape[0] // planes // 2, grad.shape[1])
        theirs = swap_cores(lax.dynamic_index_in_dim(halves, 1 - core, 1, keepdims=False))
        mine = lax.dynamic_index_in_dim(halves, core, 1, keepdims=False)
        sums.append((mine.astype(F32) + theirs.astype(F32)).astype(BF))
    return jnp.concatenate(sums, axis=2)


def sum_planes(grad):
    summed = lax.psum_scatter(grad, "dp", scatter_dimension=0, tiled=True)
    return summed.reshape(summed.shape[1:])


def normalize(values):
    center = values - jnp.mean(values, axis=-1, keepdims=True)
    spread = jnp.mean(center * center, axis=-1, keepdims=True)
    scale = lax.rsqrt(spread + NORM_EPS)
    return (center * scale, scale)


def modulate(values, shift, scale):
    return normalize(values)[0] * (1.0 + scale) + shift


def modulate_back_kernel(
    own, first, second, third, values_ref, residual, branch, scale, gate, grad_out, low_out, sums_out
):
    grad = own[...].astype(F32) + first[...].astype(F32)
    grad = grad + second[...].astype(F32) + third[...].astype(F32)
    unit, inverse = normalize(values_ref[...])
    inner = grad * (1.0 + scale[...])
    mean_one = jnp.mean(inner, axis=-1, keepdims=True)
    mean_two = jnp.mean(inner * unit, axis=-1, keepdims=True)
    result = (inner - mean_one - unit * mean_two) * inverse + residual[...]
    grad_out[...] = result
    low_out[...] = (result * gate[...]).astype(BF)
    sums_out[0:1, :] = jnp.sum(grad, axis=0, keepdims=True)
    sums_out[1:2, :] = jnp.sum(grad * unit, axis=0, keepdims=True)
    sums_out[2:3, :] = jnp.sum(result * branch[...], axis=0, keepdims=True)


def modulate_back(parts, values, residual, branch, scale, gate):
    rows, width = values.shape
    whole = pl.BlockSpec(memory_space=pltpu.VMEM)
    return pl.pallas_call(
        modulate_back_kernel,
        out_shape=(
            jax.ShapeDtypeStruct((rows, width), F32),
            jax.ShapeDtypeStruct((rows, width), BF),
            jax.ShapeDtypeStruct((8, width), F32),
        ),
        in_specs=[whole] * 9,
        out_specs=(whole, whole, whole),
        compiler_params=pltpu.CompilerParams(vmem_limit_bytes=16 * 2**20),
        cost_estimate=pl.CostEstimate(
            flops=30 * rows * width, bytes_accessed=26 * rows * width, transcendentals=rows
        ),
    )(*parts, values, residual, branch, scale, gate)


def feed_both_kernel(normed, up_ref, down_ref, down_in, act_out, grad_out, part_out, total):
    step = pl.program_id(0)
    up_value = jnp.dot(normed[...], up_ref[...], preferred_element_type=F32)
    inner = math.sqrt(2.0 / math.pi) * (up_value + 0.044715 * up_value * up_value * up_value)
    bend = jnp.tanh(inner)
    act_out[...] = (0.5 * up_value * (1.0 + bend)).astype(BF)
    slope = math.sqrt(2.0 / math.pi) * (1.0 + 3 * 0.044715 * up_value * up_value)
    slope = 0.5 * (1.0 + bend) + 0.5 * up_value * (1.0 - bend * bend) * slope
    act_grad = jnp.dot(down_in[...], down_ref[...], preferred_element_type=F32)
    up_grad = (slope * act_grad).astype(BF)
    grad_out[...] = up_grad
    part = mm_nt(up_grad, up_ref[...])

    @pl.when(step == 0)
    def _():
        total[...] = part

    @pl.when(step > 0)
    def _():
        total[...] += part

    @pl.when(step == pl.num_programs(0) - 1)
    def _():
        part_out[...] = total[...].astype(BF)


def feed_both(normed, feed, down_in):
    rows, width = normed.shape
    units = feed.shape[1] // 2
    tile = units // 3
    return pl.pallas_call(
        feed_both_kernel,
        grid=(3,),
        out_shape=(
            jax.ShapeDtypeStruct((rows, units), BF),
            jax.ShapeDtypeStruct((rows, units), BF),
            jax.ShapeDtypeStruct((rows, width), BF),
        ),
        in_specs=[
            pl.BlockSpec((rows, width), lambda j: (0, 0)),
            pl.BlockSpec((width, tile), lambda j: (0, j)),
            pl.BlockSpec((width, tile), lambda j: (0, j + 3)),
            pl.BlockSpec((rows, width), lambda j: (0, 0)),
        ],
        out_specs=(
            pl.BlockSpec((rows, tile), lambda j: (0, j)),
            pl.BlockSpec((rows, tile), lambda j: (0, j)),
            pl.BlockSpec((rows, width), lambda j: (0, 0)),
        ),
        scratch_shapes=[pltpu.VMEM((rows, width), F32)],
        compiler_params=pltpu.CompilerParams(
            dimension_semantics=("arbitrary",), vmem_limit_bytes=32 * 2**20
        ),
        cost_estimate=pl.CostEstimate(
            flops=6 * rows * width * units,
            bytes_accessed=4 * width * units + 10 * rows * width,
            transcendentals=rows * units,
        ),
    )(normed, feed, feed, down_in)


def gelu_tanh(values):
    return jax.nn.gelu(values, approximate=True)


def time_embed(steps_in, model_width):
    half_width = model_width // 2
    frequency = jnp.exp(-math.log(10000.0) * jnp.arange(half_width, dtype=F32) / half_width)
    angles = steps_in.astype(F32)[:, None] * frequency[None, :]
    return jnp.concatenate([jnp.cos(angles), jnp.sin(angles)], axis=-1)


def split_heads(stacked):
    rows, width = stacked.shape
    parts = stacked.reshape(rows, 3, width // 3 // HEAD_DIM, HEAD_DIM)
    return parts[:, 0], parts[:, 1], parts[:, 2]


def scores_of(queries, keys_in, live):
    scores = jnp.einsum("qhe,khe->hqk", queries, keys_in, preferred_element_type=F32)
    return jnp.where(live[None, None, :] > 0, scores * HEAD_DIM ** (-0.5), MASK_SCORE)


def attend(stacked, live):
    queries, keys_in, values = split_heads(stacked)
    scores = scores_of(queries, keys_in, live)
    row_peak = jnp.max(scores, axis=-1, keepdims=True)
    exponent = jnp.exp(scores - row_peak)
    row_total = jnp.sum(exponent, axis=-1, keepdims=True)
    probability = (exponent / row_total).astype(BF)
    attended = jnp.einsum("hqk,khe->qhe", probability, values, preferred_element_type=F32)
    return attended.astype(BF).reshape(stacked.shape[0], -1), row_peak + jnp.log(row_total)


def attend_back(attended_grad, stacked, live, log_total):
    rows = stacked.shape[0]
    queries, keys_in, values = split_heads(stacked)
    grad = attended_grad.reshape(values.shape)
    soft = jnp.exp(scores_of(queries, keys_in, live) - log_total)
    value_grad = jnp.einsum("hqk,qhe->khe", soft.astype(BF), grad, preferred_element_type=F32)
    prob_grad = jnp.einsum("qhe,khe->hqk", grad, values, preferred_element_type=F32)
    score_grad = soft * (prob_grad - jnp.sum(soft * prob_grad, axis=-1, keepdims=True))
    score_grad = score_grad.astype(BF)
    scale = HEAD_DIM ** (-0.5)
    query_grad = jnp.einsum("hqk,khe->qhe", score_grad, keys_in, preferred_element_type=F32) * scale
    key_grad = jnp.einsum("hqk,qhe->khe", score_grad, queries, preferred_element_type=F32) * scale
    stacked_grad = jnp.stack([query_grad, key_grad, value_grad], axis=1).astype(BF)
    return stacked_grad.reshape(rows, -1)


def block_attention(inputs, mod, live, w_attn, own_count):
    columns = w_attn.shape[1] // 4
    shift_a, scale_a, gate_a, shift_b, scale_b = (mod[i][None] for i in range(5))
    normed = modulate(inputs, shift_a, scale_a).astype(BF)
    stacked = mm(normed, w_attn[:, : 3 * columns], BF)
    attended, log_total = attend(stacked, live)
    branch_a = sum_rows(mm_nt(attended, w_attn[:, 3 * columns :], BF))
    hidden = inputs[:own_count] + gate_a * branch_a
    normed_b = gather_rows(modulate(hidden, shift_b, scale_b).astype(BF))
    padded = jnp.pad(attended, ((0, 0), (3 * columns, 0)))
    normed_b, padded = tie(normed_b, padded)
    return (normed, stacked, padded, log_total, branch_a, hidden, normed_b)


def block_back_feed(up_grad, partial, down_in, activated, grad_own, mod, saved, core):
    hidden, normed_b, branch_a = saved
    partial, up_grad, down_in, activated = tie(partial, up_grad, down_in, activated)
    grad_down = mm_tn(down_in, activated, BF)
    grad_up = mm_tn(normed_b, up_grad, BF)
    parts, grads = tie(spread_rows(partial), sum_cores(core, grad_up, grad_down))
    feed_sum = sum_planes(grads)
    return modulate_back(parts, hidden, grad_own, branch_a, mod[4][None], mod[2][None]), feed_sum


def block_back_attention(output_in, hidden_grad, inputs_own, mod, live, saved, w_attn, core):
    normed, stacked, padded, log_total = saved
    columns = w_attn.shape[1] // 4
    attended_grad = mm(output_in, w_attn[:, 3 * columns :], BF)
    stacked_grad = attend_back(attended_grad, stacked, live, log_total)
    partial = mm_nt(stacked_grad, w_attn[:, : 3 * columns], BF)
    partial, stacked_grad, output_in = tie(partial, stacked_grad, output_in)
    lefts = jnp.concatenate([normed, output_in], axis=0)
    wide_grad = jnp.pad(stacked_grad, ((0, 0), (0, columns)))
    grad_attn = mm_tn(lefts, jnp.concatenate([wide_grad, padded], axis=0), BF)
    parts, grad_attn = tie(spread_rows(partial), sum_cores(core, grad_attn))
    attn_sum = sum_planes(grad_attn)
    return parts, attn_sum


def squared(values):
    wide = values.astype(F32)
    return jnp.sum(wide * wide)


def adam_update(weight_in, first_in, second_in, gradient, factor):
    clipped = gradient * factor
    first_out = BETA_ONE * first_in + (1.0 - BETA_ONE) * clipped
    second_out = BETA_TWO * second_in + (1.0 - BETA_TWO) * clipped * clipped
    ratio = (
        first_out
        / (1.0 - BETA_ONE**STEP)
        / (jnp.sqrt(second_out / (1.0 - BETA_TWO**STEP)) + ADAM_EPS)
    )
    weight_out = weight_in - LEARN_RATE * (ratio + WEIGHT_DECAY * weight_in)
    return (weight_out, first_out, second_out)


def per_device(
    tokens,
    cotangent,
    kept_index,
    full_flag,
    labels,
    timesteps,
    class_table,
    heads_weight,
    heads_first,
    heads_second,
    output_weight,
    output_first,
    output_second,
    up_weight,
    up_first,
    up_second,
    down_weight,
    down_first,
    down_second,
    adaln_weight,
    adaln_first,
    adaln_second,
    mask_token,
    mask_first,
    mask_second,
):
    image_count, seq_length, model_width = tokens.shape
    section = lax.axis_index("section")
    core = lax.axis_index("core")
    plane = lax.axis_index("dp")
    chip = lax.axis_index("row") * 2 + section
    quarter = seq_length // 4
    shard = model_width // lax.axis_size("dp")
    columns = heads_weight.shape[-1]

    with jax.named_scope("weights_in"):
        attn_pack = jnp.concatenate(
            [heads_weight[0, 0], heads_weight[0, 1], heads_weight[0, 2], output_weight[0].T], axis=1
        ).astype(BF)
        *halves, feed_parts = send_shares(attn_pack, section, core, (up_weight[0], down_weight[0]))
        attn_half = jnp.concatenate(halves, axis=1)
        feed_pack = jnp.concatenate([feed_parts[0], feed_parts[1].T], axis=1).astype(BF)
        feed_pack, attn_half = tie(feed_pack, attn_half)
        attn_all = gather_weight(attn_half)
        attn_width = attn_pack.shape[1]
        enc_attn, dec_attn = attn_all[:, :attn_width], attn_all[:, attn_width:]
        enc_feed_half, dec_feed_half, _ = send_shares(feed_pack, section, core)
        feed_width = feed_pack.shape[1] // 2
        enc_feed = gather_weight(enc_feed_half)

    with jax.named_scope("modulation"):
        codes = planes_gather(jnp.stack([labels, timesteps], axis=1))
        class_count = class_table.shape[0]
        label_hot = (codes[:, :1] == jnp.arange(class_count, dtype=jnp.int32)[None, :]).astype(BF)
        condition = mm(label_hot, class_table) + time_embed(codes[:, 1], model_width)
        cond_act = jax.nn.silu(condition).astype(BF)
        cond_rows = lax.dynamic_slice_in_dim(cond_act, plane * shard, shard, 1)
        adaln_part = planes_sum(mm(cond_rows, adaln_weight[0].astype(BF)))
        adaln_all = lax.all_gather(adaln_part, PLANE, axis=0, tiled=False)
        mod_all = lax.dynamic_index_in_dim(adaln_all, core, 1, keepdims=False)
        mod_all = mod_all.reshape(2, 6, model_width)
        enc_mod, dec_mod = mod_all[0], mod_all[1]

    def relative(values):
        parts = [
            lax.dynamic_slice_in_dim(values, (chip ^ offset) * quarter, quarter, 0)
            for offset in range(4)
        ]
        return jnp.concatenate(parts, axis=0)

    with jax.named_scope("placement"):
        image_tokens = lax.dynamic_index_in_dim(tokens, core, 0, keepdims=False)
        image_cot = relative(lax.dynamic_index_in_dim(cotangent, core, 0, keepdims=False))
        kept = relative(lax.dynamic_index_in_dim(kept_index, core, 0, keepdims=False))
        flag = lax.dynamic_index_in_dim(full_flag, core, 0, keepdims=False)
        plain_ids = jnp.arange(seq_length, dtype=jnp.int32)
        ids = ((plain_ids // quarter) ^ chip) * quarter + plain_ids % quarter
        live = ids < jnp.where(flag > 0, seq_length, seq_length // 2)
        place_plain = ((kept[:, None] == plain_ids[None, :]) & live[:, None]).astype(BF)
        place = ((kept[:, None] == ids[None, :]) & live[:, None]).astype(BF)
        live = live.astype(F32)
        uncovered = 1.0 - jnp.sum(place.astype(F32), axis=0)
        restore = (ids[:, None] == plain_ids[None, :]).astype(BF)
        enc_in = mm(place_plain, image_tokens)

    def feed_up(normed_b, feed):
        up_value = mm(normed_b, feed[:, :feed_width])
        return up_value, gelu_tanh(up_value).astype(BF)

    def feed_down(activated, feed):
        return sum_rows(mm_nt(activated, feed[:, feed_width:], BF))

    with jax.named_scope("encoder"):
        normed, stacked, attended, log_total, branch_a, hidden, normed_b = block_attention(
            enc_in, enc_mod, live, enc_attn, quarter
        )
        normed_b, dec_feed_half = tie(normed_b, dec_feed_half)
        dec_feed = gather_weight(dec_feed_half)
        enc_up_value, enc_act = feed_up(normed_b, enc_feed)
        branch_b = feed_down(enc_act, enc_feed)
        enc_branch_b = branch_b
        enc_out = (hidden + enc_mod[5][None] * branch_b) * live[:quarter, None]
        sent = gather_rows(enc_out.astype(BF))
        enc_attn_saved = (normed, stacked, attended, log_total)
        enc_feed_saved = (hidden, normed_b, branch_a)

    with jax.named_scope("decoder"):
        dec_in = mm_tn(place, sent) + uncovered[:, None] * mask_token[None, :]
        all_live = jnp.ones_like(live)
        normed, stacked, attended, log_total, branch_a, hidden, normed_b = block_attention(
            dec_in, dec_mod, all_live, dec_attn, quarter
        )
        dec_down_in = (dec_mod[5][None] * image_cot.astype(F32)).astype(BF)
        dec_act, dec_up_grad, dec_partial = feed_both(normed_b, dec_feed, dec_down_in)
        dec_attn_saved = (normed, stacked, attended, log_total)
        dec_feed_saved = (hidden, normed_b, branch_a)

    is_first = section == 0

    def both_images(mine):
        other = swap_cores(mine)
        pair = jnp.where(core == 0, jnp.stack([mine, other]), jnp.stack([other, mine]))
        return pair[None]

    ones = jnp.ones((1, model_width), F32)

    with jax.named_scope("decoder_back"):
        (hidden_grad, output_in, mods_b), dec_feed_sum = block_back_feed(
            dec_up_grad,
            dec_partial,
            dec_down_in,
            dec_act,
            image_cot[:quarter].astype(F32),
            dec_mod,
            dec_feed_saved,
            core,
        )
        output_in = gather_rows(output_in)
        parts, dec_attn_sum = block_back_attention(
            output_in,
            hidden_grad,
            dec_in[:quarter],
            dec_mod,
            all_live,
            dec_attn_saved,
            dec_attn,
            core,
        )
        parts, dec_feed_sum = tie(parts, dec_feed_sum)
        dec_grad, dec_low, mods_a = modulate_back(
            parts,
            dec_in[:quarter],
            hidden_grad,
            jnp.broadcast_to(uncovered[:quarter, None], hidden_grad.shape),
            dec_mod[1][None],
            ones,
        )
        mask_part = mods_a[2]
        dec_mods = (mods_a[0:2], mods_b[2:3], mods_b[0:2])
        dec_low = gather_rows(dec_low)

    with jax.named_scope("encoder_back"):
        enc_cot = mm(place, dec_low)
        down_in = (enc_mod[5][None] * enc_cot).astype(BF)
        act_grad = mm(down_in, enc_feed[:, feed_width:])
        up_grad = jax.vjp(gelu_tanh, enc_up_value)[1](act_grad)[0].astype(BF)
        partial = mm_nt(up_grad, enc_feed[:, :feed_width], BF)
        partial, dec_act = tie(partial, dec_act)
        (hidden_grad, output_in, mods_b), enc_feed_sum = block_back_feed(
            up_grad,
            partial,
            down_in,
            enc_act,
            enc_cot[:quarter],
            enc_mod,
            enc_feed_saved,
            core,
        )
        output_in, dec_attn_sum = tie(output_in, dec_attn_sum)
        output_in = gather_rows(output_in)
        branch_b = feed_down(dec_act, dec_feed)
        dec_out = dec_feed_saved[0] + dec_mod[5][None] * branch_b
        gate_grad = jnp.sum(image_cot[:quarter].astype(F32) * branch_b, axis=0, keepdims=True)
        dec_mods = dec_mods + (gate_grad,)
        enc_gate_grad = jnp.sum(enc_cot[:quarter] * enc_branch_b, axis=0, keepdims=True)
        dec_out = gather_rows(dec_out.astype(BF))
        layer_out = both_images(mm_tn(restore, jnp.where(is_first, sent, dec_out), BF))
        parts, enc_attn_sum = block_back_attention(
            output_in,
            hidden_grad,
            enc_in[:quarter],
            enc_mod,
            live,
            enc_attn_saved,
            enc_attn,
            core,
        )
        parts, enc_feed_sum, layer_out = tie(parts, enc_feed_sum, layer_out)
        _, enc_low, mods_a = modulate_back(
            parts, enc_in[:quarter], hidden_grad, hidden_grad, enc_mod[1][None], ones
        )
        enc_low = gather_rows(enc_low)
        enc_mods = (mods_a[0:2], mods_b[2:3], mods_b[0:2], enc_gate_grad)

    with jax.named_scope("modulation_back"):
        mod_parts = jnp.concatenate(enc_mods + dec_mods, axis=0)
        mod_parts = lax.all_to_all(mod_parts.reshape(8, -1), PLANE, 0, 0, tiled=True)
        mod_parts, enc_feed_sum, enc_low = tie(mod_parts, enc_feed_sum, enc_low)
        mod_grad = planes_gather(jnp.sum(mod_parts.reshape(4, 2, -1), axis=0))

    with jax.named_scope("outputs"):
        arrange = jnp.where(is_first, place_plain, restore)
        in_grads = both_images(mm_tn(arrange, jnp.where(is_first, enc_low, dec_low), BF))

    with jax.named_scope("returns"):
        keep, given = return_over_section(enc_feed_sum, dec_feed_sum, section)

    with jax.named_scope("modulation_back"):
        grad_adaln = lax.dot_general(
            cond_rows.astype(F32), mod_grad, (((0,), (0,)), ((), ())), precision=PRECISE
        )

    with jax.named_scope("norm"):
        square = jnp.sum(grad_adaln * grad_adaln)
        for part in (dec_attn_sum, dec_feed_sum, enc_feed_sum):
            square = square + squared(part)
        square, grad_adaln, keep, given, in_grads, dec_attn_sum, enc_attn_sum = tie(
            square, grad_adaln, keep, given, in_grads, dec_attn_sum, enc_attn_sum
        )
        feed_grad = return_over_core(keep, given, section, core)
        down_grad = turned(feed_grad[:, feed_width:])
        up_grad = feed_grad[:, :feed_width]
        square = square + squared(enc_attn_sum)
        totals = jnp.concatenate([mask_part, jnp.full((128,), square / 128.0, F32)])
        totals = sum_over(totals.reshape(1, -1), ("dp",))
        keep, given = return_over_section(enc_attn_sum, dec_attn_sum, section)
        totals, keep, given = tie(totals, keep, given)
        totals = sum_over(totals, ("row", "section", "core"))[0]
        attn_grad = return_over_core(keep, given, section, core)
        heads_grad = jnp.stack([attn_grad[:, i * columns : (i + 1) * columns] for i in range(3)])
        output_grad = turned(attn_grad[:, 3 * columns :])
        totals, heads_grad, output_grad, up_grad, down_grad = tie(
            totals, heads_grad, output_grad, up_grad, down_grad
        )
        mask_total = totals[:model_width]
        grad_norm = jnp.sqrt(jnp.sum(totals[model_width:]) + jnp.sum(mask_total * mask_total))
        factor = jnp.minimum(1.0, CLIP_NORM / (grad_norm + NORM_EPS))

    with jax.named_scope("update"):
        gradients = [
            part.astype(F32)[None] for part in (heads_grad, output_grad, up_grad, down_grad)
        ] + [grad_adaln[None]]
        masters = (heads_weight, output_weight, up_weight, down_weight, adaln_weight)
        firsts = (heads_first, output_first, up_first, down_first, adaln_first)
        seconds = (heads_second, output_second, up_second, down_second, adaln_second)
        updated = []
        for position in range(5):
            updated += adam_update(
                masters[position], firsts[position], seconds[position], gradients[position], factor
            )
        mask_next = adam_update(mask_token, mask_first, mask_second, mask_total, factor)

    return (layer_out, in_grads, *updated, *mask_next, grad_norm)


def solution(mesh):
    sizes = dict(mesh.shape)
    parted = Mesh(
        mesh.devices.reshape(sizes["section"], sizes["tensor"] // 2, 2, sizes["dp"]),
        ("section", "row", "core", "dp"),
    )
    tensor = ("row", "core")
    heads = P("section", None, "dp", tensor)
    tensor_dp = P("section", tensor, "dp")
    dp_tensor = P("section", "dp", tensor)
    weights = [heads] * 3 + [tensor_dp] * 3 + [dp_tensor] * 3 + [tensor_dp] * 3 + [dp_tensor] * 3
    images = P("dp", None, None)
    layers = P("section", "dp", None, None)
    return jax.shard_map(
        per_device,
        mesh=parted,
        in_specs=(
            images,
            images,
            P("dp", None),
            P("dp"),
            P("dp"),
            P("dp"),
            P(),
            *weights,
            P(),
            P(),
            P(),
        ),
        out_specs=(layers, layers, *weights, P(), P(), P(), P()),
        check_vma=False,
    )
```

```python
import math

import jax
import jax.numpy as jnp
from jax import lax
from jax.experimental import pallas as pl
from jax.experimental.pallas import tpu as pltpu
from jax.sharding import Mesh
from jax.sharding import PartitionSpec as P

HEAD_DIM = 72
STEP = 10

PRECISE = lax.Precision.HIGHEST
NORM_EPS = 1e-06
BETA_ONE = 0.9
BETA_TWO = 0.99
LEARN_RATE = 0.05
WEIGHT_DECAY = 0.01
ADAM_EPS = 1e-08
CLIP_NORM = 1.0
MASK_SCORE = -1000000000.0

BF = jnp.bfloat16
F32 = jnp.float32
PLANE = ("section", "row", "core")
CHIPS = ("section", "row")
ROWS_BY = ("dp", "core")


def dot(left, right, dims, out=F32):
    return lax.dot_general(left, right, (dims, ((), ())), preferred_element_type=F32).astype(out)


def mm(left, right, out=F32):
    return dot(left, right, ((1,), (0,)), out)


def mm_nt(left, right, out=F32):
    return dot(left, right, ((1,), (1,)), out)


def mm_tn(left, right, out=F32):
    return dot(left, right, ((0,), (0,)), out)


def turned(values):
    return mm_tn(values, jnp.eye(values.shape[0], dtype=values.dtype), values.dtype)


def chip_route(offset):
    return [
        (s * 2 + r, (s ^ (offset & 1)) * 2 + (r ^ (offset >> 1)))
        for s in range(2)
        for r in range(2)
    ]


def swap_chips(block, offset):
    return lax.ppermute(block, CHIPS, chip_route(offset))


def swap_cores(block):
    return lax.ppermute(block, "core", [(0, 1), (1, 0)])


def gather_rows(own):
    return jnp.concatenate([own] + [swap_chips(own, offset) for offset in (1, 2, 3)], axis=0)


def spread_rows(partial):
    count = partial.shape[0] // 4
    parts = [
        swap_chips(partial[offset * count : (offset + 1) * count], offset) for offset in (3, 2, 1)
    ]
    return [partial[:count]] + parts


def sum_rows(partial):
    return sum(part.astype(F32) for part in spread_rows(partial))


def xor_route(size, offset):
    return [(i, i ^ offset) for i in range(size)]


def planes_gather(block):
    size = lax.axis_size("dp")
    parts = [block] + [
        lax.ppermute(block, "dp", xor_route(size, offset)) for offset in range(1, size)
    ]
    return jnp.concatenate(parts, axis=0)


def planes_sum(blocks):
    size = lax.axis_size("dp")
    count = blocks.shape[0] // size
    total = blocks[:count]
    for offset in range(1, size):
        part = blocks[offset * count : (offset + 1) * count]
        total = total + lax.ppermute(part, "dp", xor_route(size, offset))
    return total


def sum_over(values, axes):
    for axis in axes:
        size = lax.axis_size(axis)
        step = 1
        while step < size:
            values = values + lax.ppermute(values, axis, xor_route(size, step))
            step *= 2
    return values


def send_shares(pack, section, core):
    half = pack.shape[0] // 2
    mine = lax.dynamic_slice_in_dim(pack, core * half, half, 0)
    other = swap_cores(lax.dynamic_slice_in_dim(pack, (1 - core) * half, half, 0))
    keep = jnp.where(core == section, mine, other)
    give = jnp.where(core == section, other, mine)
    return keep, lax.ppermute(give, "section", [(0, 1), (1, 0)])


def by_block(keep, given, section):
    return (jnp.where(section == 0, keep, given), jnp.where(section == 0, given, keep))


def assemble_kernel(order_ref, mine_ref, other_ref, out_ref):
    count = mine_ref.shape[1]
    for part in range(4):
        for which, source in enumerate((mine_ref, other_ref)):
            start = pl.multiple_of(order_ref[which * 4 + part] * count, count)
            out_ref[pl.ds(start, count), :] = source[part]


def assemble(parts, plane, core):
    mine = jnp.stack(parts)
    other = swap_cores(mine)
    planes = jnp.stack([plane ^ offset for offset in range(4)]).astype(jnp.int32)
    order = jnp.concatenate([planes * 2 + core, planes * 2 + 1 - core])
    whole = pl.BlockSpec(memory_space=pltpu.VMEM)
    return pl.pallas_call(
        assemble_kernel,
        out_shape=jax.ShapeDtypeStruct((8 * mine.shape[1], mine.shape[2]), mine.dtype),
        in_specs=[pl.BlockSpec(memory_space=pltpu.SMEM), whole, whole],
        out_specs=whole,
        compiler_params=pltpu.CompilerParams(vmem_limit_bytes=24 * 2**20),
        cost_estimate=pl.CostEstimate(
            flops=0, bytes_accessed=8 * mine.size, transcendentals=0
        ),
    )(order, mine, other)


def return_over_section(first, second, section):
    keep = jnp.where(section == 0, first, second)
    give = jnp.where(section == 0, second, first)
    return (keep, lax.ppermute(give, "section", [(0, 1), (1, 0)]))


def return_over_core(keep, given, section, core):
    mine = jnp.where(core == section, keep, given)
    other = swap_cores(jnp.where(core == section, given, keep))
    top = jnp.where(core == 0, mine, other)
    bottom = jnp.where(core == 0, other, mine)
    return jnp.concatenate([top, bottom], axis=0)


def tie(*values):
    return lax.optimization_barrier(values)


def gather_weight(half):
    return lax.all_gather(half, ROWS_BY, axis=0, tiled=True)


def sum_cores(core, *grads):
    planes = lax.axis_size("dp")
    sums = []
    for grad in grads:
        halves = grad.reshape(planes, 2, grad.shape[0] // planes // 2, grad.shape[1])
        theirs = swap_cores(lax.dynamic_index_in_dim(halves, 1 - core, 1, keepdims=False))
        mine = lax.dynamic_index_in_dim(halves, core, 1, keepdims=False)
        sums.append((mine.astype(F32) + theirs.astype(F32)).astype(BF))
    return jnp.concatenate(sums, axis=2)


def sum_planes(grad):
    summed = lax.psum_scatter(grad, "dp", scatter_dimension=0, tiled=True)
    return summed.reshape(summed.shape[1:])


def normalize(values):
    center = values - jnp.mean(values, axis=-1, keepdims=True)
    spread = jnp.mean(center * center, axis=-1, keepdims=True)
    scale = lax.rsqrt(spread + NORM_EPS)
    return (center * scale, scale)


def modulate(values, shift, scale):
    return normalize(values)[0] * (1.0 + scale) + shift


def modulate_back_kernel(
    own, first, second, third, values_ref, residual, branch, scale, gate, grad_out, low_out, sums_out
):
    grad = own[...].astype(F32) + first[...].astype(F32)
    grad = grad + second[...].astype(F32) + third[...].astype(F32)
    unit, inverse = normalize(values_ref[...])
    inner = grad * (1.0 + scale[...])
    mean_one = jnp.mean(inner, axis=-1, keepdims=True)
    mean_two = jnp.mean(inner * unit, axis=-1, keepdims=True)
    result = (inner - mean_one - unit * mean_two) * inverse + residual[...]
    grad_out[...] = result
    low_out[...] = (result * gate[...]).astype(BF)
    sums_out[0:1, :] = jnp.sum(grad, axis=0, keepdims=True)
    sums_out[1:2, :] = jnp.sum(grad * unit, axis=0, keepdims=True)
    sums_out[2:3, :] = jnp.sum(result * branch[...], axis=0, keepdims=True)


def modulate_back(parts, values, residual, branch, scale, gate):
    rows, width = values.shape
    whole = pl.BlockSpec(memory_space=pltpu.VMEM)
    return pl.pallas_call(
        modulate_back_kernel,
        out_shape=(
            jax.ShapeDtypeStruct((rows, width), F32),
            jax.ShapeDtypeStruct((rows, width), BF),
            jax.ShapeDtypeStruct((8, width), F32),
        ),
        in_specs=[whole] * 9,
        out_specs=(whole, whole, whole),
        compiler_params=pltpu.CompilerParams(vmem_limit_bytes=16 * 2**20),
        cost_estimate=pl.CostEstimate(
            flops=30 * rows * width, bytes_accessed=26 * rows * width, transcendentals=rows
        ),
    )(*parts, values, residual, branch, scale, gate)


def feed_both_kernel(normed, up_ref, down_ref, down_in, act_out, grad_out, part_out, total):
    step = pl.program_id(0)
    up_value = jnp.dot(normed[...], up_ref[...], preferred_element_type=F32)
    inner = math.sqrt(2.0 / math.pi) * (up_value + 0.044715 * up_value * up_value * up_value)
    bend = jnp.tanh(inner)
    act_out[...] = (0.5 * up_value * (1.0 + bend)).astype(BF)
    slope = math.sqrt(2.0 / math.pi) * (1.0 + 3 * 0.044715 * up_value * up_value)
    slope = 0.5 * (1.0 + bend) + 0.5 * up_value * (1.0 - bend * bend) * slope
    act_grad = jnp.dot(down_in[...], down_ref[...], preferred_element_type=F32)
    up_grad = (slope * act_grad).astype(BF)
    grad_out[...] = up_grad
    part = mm_nt(up_grad, up_ref[...])

    @pl.when(step == 0)
    def _():
        total[...] = part

    @pl.when(step > 0)
    def _():
        total[...] += part

    @pl.when(step == pl.num_programs(0) - 1)
    def _():
        part_out[...] = total[...].astype(BF)


def feed_both(normed, feed, down_in):
    rows, width = normed.shape
    units = feed.shape[1] // 2
    tile = units // 3
    return pl.pallas_call(
        feed_both_kernel,
        grid=(3,),
        out_shape=(
            jax.ShapeDtypeStruct((rows, units), BF),
            jax.ShapeDtypeStruct((rows, units), BF),
            jax.ShapeDtypeStruct((rows, width), BF),
        ),
        in_specs=[
            pl.BlockSpec((rows, width), lambda j: (0, 0)),
            pl.BlockSpec((width, tile), lambda j: (0, j)),
            pl.BlockSpec((width, tile), lambda j: (0, j + 3)),
            pl.BlockSpec((rows, width), lambda j: (0, 0)),
        ],
        out_specs=(
            pl.BlockSpec((rows, tile), lambda j: (0, j)),
            pl.BlockSpec((rows, tile), lambda j: (0, j)),
            pl.BlockSpec((rows, width), lambda j: (0, 0)),
        ),
        scratch_shapes=[pltpu.VMEM((rows, width), F32)],
        compiler_params=pltpu.CompilerParams(
            dimension_semantics=("arbitrary",), vmem_limit_bytes=32 * 2**20
        ),
        cost_estimate=pl.CostEstimate(
            flops=6 * rows * width * units,
            bytes_accessed=4 * width * units + 10 * rows * width,
            transcendentals=rows * units,
        ),
    )(normed, feed, feed, down_in)


def gelu_tanh(values):
    return jax.nn.gelu(values, approximate=True)


def time_embed(steps_in, model_width):
    half_width = model_width // 2
    frequency = jnp.exp(-math.log(10000.0) * jnp.arange(half_width, dtype=F32) / half_width)
    angles = steps_in.astype(F32)[:, None] * frequency[None, :]
    return jnp.concatenate([jnp.cos(angles), jnp.sin(angles)], axis=-1)


def split_heads(stacked):
    rows, width = stacked.shape
    parts = stacked.reshape(rows, 3, width // 3 // HEAD_DIM, HEAD_DIM)
    return parts[:, 0], parts[:, 1], parts[:, 2]


def scores_of(queries, keys_in, live):
    scores = jnp.einsum("qhe,khe->hqk", queries, keys_in, preferred_element_type=F32)
    return jnp.where(live[None, None, :] > 0, scores * HEAD_DIM ** (-0.5), MASK_SCORE)


def attend(stacked, live):
    queries, keys_in, values = split_heads(stacked)
    scores = scores_of(queries, keys_in, live)
    row_peak = jnp.max(scores, axis=-1, keepdims=True)
    exponent = jnp.exp(scores - row_peak)
    row_total = jnp.sum(exponent, axis=-1, keepdims=True)
    probability = (exponent / row_total).astype(BF)
    attended = jnp.einsum("hqk,khe->qhe", probability, values, preferred_element_type=F32)
    return attended.astype(BF).reshape(stacked.shape[0], -1), row_peak + jnp.log(row_total)


def attend_back(attended_grad, stacked, live, log_total):
    rows = stacked.shape[0]
    queries, keys_in, values = split_heads(stacked)
    grad = attended_grad.reshape(values.shape)
    soft = jnp.exp(scores_of(queries, keys_in, live) - log_total)
    value_grad = jnp.einsum("hqk,qhe->khe", soft.astype(BF), grad, preferred_element_type=F32)
    prob_grad = jnp.einsum("qhe,khe->hqk", grad, values, preferred_element_type=F32)
    score_grad = soft * (prob_grad - jnp.sum(soft * prob_grad, axis=-1, keepdims=True))
    score_grad = score_grad.astype(BF)
    scale = HEAD_DIM ** (-0.5)
    query_grad = jnp.einsum("hqk,khe->qhe", score_grad, keys_in, preferred_element_type=F32) * scale
    key_grad = jnp.einsum("hqk,qhe->khe", score_grad, queries, preferred_element_type=F32) * scale
    stacked_grad = jnp.stack([query_grad, key_grad, value_grad], axis=1).astype(BF)
    return stacked_grad.reshape(rows, -1)


def block_attention(inputs, mod, live, w_attn, own_count):
    columns = w_attn.shape[1] // 4
    shift_a, scale_a, gate_a, shift_b, scale_b = (mod[i][None] for i in range(5))
    normed = modulate(inputs, shift_a, scale_a).astype(BF)
    stacked = mm(normed, w_attn[:, : 3 * columns], BF)
    attended, log_total = attend(stacked, live)
    branch_a = sum_rows(mm_nt(attended, w_attn[:, 3 * columns :], BF))
    hidden = inputs[:own_count] + gate_a * branch_a
    normed_b = gather_rows(modulate(hidden, shift_b, scale_b).astype(BF))
    padded = jnp.pad(attended, ((0, 0), (3 * columns, 0)))
    normed_b, padded = tie(normed_b, padded)
    return (normed, stacked, padded, log_total, branch_a, hidden, normed_b)


def block_back_feed(up_grad, partial, down_in, activated, grad_own, mod, saved, core, late):
    hidden, normed_b, branch_a = saved
    partial, up_grad, down_in, activated = tie(partial, up_grad, down_in, activated)
    grad_down = mm_tn(down_in, activated, BF)
    grad_up = mm_tn(normed_b, up_grad, BF)
    grads = sum_cores(core, grad_up, grad_down)
    if late:
        parts, grads = tie(spread_rows(partial), grads)
    else:
        partial, grads = tie(partial, grads)
        parts = spread_rows(partial)
    feed_sum = sum_planes(grads)
    return modulate_back(parts, hidden, grad_own, branch_a, mod[4][None], mod[2][None]), feed_sum


def block_back_attention(output_in, hidden_grad, inputs_own, mod, live, saved, w_attn, core):
    normed, stacked, padded, log_total = saved
    columns = w_attn.shape[1] // 4
    attended_grad = mm(output_in, w_attn[:, 3 * columns :], BF)
    stacked_grad = attend_back(attended_grad, stacked, live, log_total)
    partial = mm_nt(stacked_grad, w_attn[:, : 3 * columns], BF)
    partial, stacked_grad, output_in = tie(partial, stacked_grad, output_in)
    lefts = jnp.concatenate([normed, output_in], axis=0)
    wide_grad = jnp.pad(stacked_grad, ((0, 0), (0, columns)))
    grad_attn = mm_tn(lefts, jnp.concatenate([wide_grad, padded], axis=0), BF)
    parts, grad_attn = tie(spread_rows(partial), sum_cores(core, grad_attn))
    attn_sum = sum_planes(grad_attn)
    return parts, attn_sum


def squared(values):
    wide = values.astype(F32)
    return jnp.sum(wide * wide)


def adam_update(weight_in, first_in, second_in, gradient, factor):
    clipped = gradient * factor
    first_out = BETA_ONE * first_in + (1.0 - BETA_ONE) * clipped
    second_out = BETA_TWO * second_in + (1.0 - BETA_TWO) * clipped * clipped
    ratio = (
        first_out
        / (1.0 - BETA_ONE**STEP)
        / (jnp.sqrt(second_out / (1.0 - BETA_TWO**STEP)) + ADAM_EPS)
    )
    weight_out = weight_in - LEARN_RATE * (ratio + WEIGHT_DECAY * weight_in)
    return (weight_out, first_out, second_out)


def per_device(
    tokens,
    cotangent,
    kept_index,
    full_flag,
    labels,
    timesteps,
    class_table,
    heads_weight,
    heads_first,
    heads_second,
    output_weight,
    output_first,
    output_second,
    up_weight,
    up_first,
    up_second,
    down_weight,
    down_first,
    down_second,
    adaln_weight,
    adaln_first,
    adaln_second,
    mask_token,
    mask_first,
    mask_second,
):
    image_count, seq_length, model_width = tokens.shape
    section = lax.axis_index("section")
    core = lax.axis_index("core")
    plane = lax.axis_index("dp")
    chip = lax.axis_index("row") * 2 + section
    quarter = seq_length // 4
    shard = model_width // lax.axis_size("dp")
    columns = heads_weight.shape[-1]

    with jax.named_scope("weights_in"):
        attn_pack = jnp.concatenate(
            [heads_weight[0, 0], heads_weight[0, 1], heads_weight[0, 2], output_weight[0].T], axis=1
        ).astype(BF)
        keep, given = send_shares(attn_pack, section, core)
        if lax.axis_size("dp") == 4:
            parts = [keep] + [lax.ppermute(keep, "dp", xor_route(4, m)) for m in (1, 2, 3)]
            given, *parts = tie(given, *parts)
            given_all = gather_weight(given)
            keep_all = assemble(parts, plane, core)
        else:
            given_all, keep_all = gather_weight(given), gather_weight(keep)
        enc_attn, dec_attn = by_block(keep_all, given_all, section)
        feed_pack = jnp.concatenate([up_weight[0], down_weight[0].T], axis=1).astype(BF)
        feed_pack, given = tie(feed_pack, given)
        enc_feed_half, dec_feed_half = by_block(*send_shares(feed_pack, section, core), section)
        feed_width = feed_pack.shape[1] // 2
        enc_feed = gather_weight(enc_feed_half)

    with jax.named_scope("modulation"):
        codes = planes_gather(jnp.stack([labels, timesteps], axis=1))
        class_count = class_table.shape[0]
        label_hot = (codes[:, :1] == jnp.arange(class_count, dtype=jnp.int32)[None, :]).astype(BF)
        condition = mm(label_hot, class_table) + time_embed(codes[:, 1], model_width)
        cond_act = jax.nn.silu(condition).astype(BF)
        cond_rows = lax.dynamic_slice_in_dim(cond_act, plane * shard, shard, 1)
        adaln_part = planes_sum(mm(cond_rows, adaln_weight[0].astype(BF)))
        adaln_all = lax.all_gather(adaln_part, PLANE, axis=0, tiled=False)
        mod_all = lax.dynamic_index_in_dim(adaln_all, core, 1, keepdims=False)
        mod_all = mod_all.reshape(2, 6, model_width)
        enc_mod, dec_mod = mod_all[0], mod_all[1]

    def relative(values):
        parts = [
            lax.dynamic_slice_in_dim(values, (chip ^ offset) * quarter, quarter, 0)
            for offset in range(4)
        ]
        return jnp.concatenate(parts, axis=0)

    with jax.named_scope("placement"):
        image_tokens = lax.dynamic_index_in_dim(tokens, core, 0, keepdims=False)
        image_cot = relative(lax.dynamic_index_in_dim(cotangent, core, 0, keepdims=False))
        kept = relative(lax.dynamic_index_in_dim(kept_index, core, 0, keepdims=False))
        flag = lax.dynamic_index_in_dim(full_flag, core, 0, keepdims=False)
        plain_ids = jnp.arange(seq_length, dtype=jnp.int32)
        ids = ((plain_ids // quarter) ^ chip) * quarter + plain_ids % quarter
        live = ids < jnp.where(flag > 0, seq_length, seq_length // 2)
        place_plain = ((kept[:, None] == plain_ids[None, :]) & live[:, None]).astype(BF)
        place = ((kept[:, None] == ids[None, :]) & live[:, None]).astype(BF)
        live = live.astype(F32)
        uncovered = 1.0 - jnp.sum(place.astype(F32), axis=0)
        restore = (ids[:, None] == plain_ids[None, :]).astype(BF)
        enc_in = mm(place_plain, image_tokens)

    def feed_up(normed_b, feed):
        up_value = mm(normed_b, feed[:, :feed_width])
        return up_value, gelu_tanh(up_value).astype(BF)

    def feed_down(activated, feed):
        return sum_rows(mm_nt(activated, feed[:, feed_width:], BF))

    with jax.named_scope("encoder"):
        normed, stacked, attended, log_total, branch_a, hidden, normed_b = block_attention(
            enc_in, enc_mod, live, enc_attn, quarter
        )
        normed_b, dec_feed_half = tie(normed_b, dec_feed_half)
        dec_feed = gather_weight(dec_feed_half)
        enc_up_value, enc_act = feed_up(normed_b, enc_feed)
        branch_b = feed_down(enc_act, enc_feed)
        enc_branch_b = branch_b
        enc_out = (hidden + enc_mod[5][None] * branch_b) * live[:quarter, None]
        sent = gather_rows(enc_out.astype(BF))
        enc_attn_saved = (normed, stacked, attended, log_total)
        enc_feed_saved = (hidden, normed_b, branch_a)

    with jax.named_scope("decoder"):
        dec_in = mm_tn(place, sent) + uncovered[:, None] * mask_token[None, :]
        all_live = jnp.ones_like(live)
        normed, stacked, attended, log_total, branch_a, hidden, normed_b = block_attention(
            dec_in, dec_mod, all_live, dec_attn, quarter
        )
        dec_down_in = (dec_mod[5][None] * image_cot.astype(F32)).astype(BF)
        dec_act, dec_up_grad, dec_partial = feed_both(normed_b, dec_feed, dec_down_in)
        dec_attn_saved = (normed, stacked, attended, log_total)
        dec_feed_saved = (hidden, normed_b, branch_a)

    is_first = section == 0

    def both_images(mine):
        other = swap_cores(mine)
        pair = jnp.where(core == 0, jnp.stack([mine, other]), jnp.stack([other, mine]))
        return pair[None]

    ones = jnp.ones((1, model_width), F32)

    with jax.named_scope("decoder_back"):
        (hidden_grad, output_in, mods_b), dec_feed_sum = block_back_feed(
            dec_up_grad,
            dec_partial,
            dec_down_in,
            dec_act,
            image_cot[:quarter].astype(F32),
            dec_mod,
            dec_feed_saved,
            core,
            False,
        )
        output_in = gather_rows(output_in)
        parts, dec_attn_sum = block_back_attention(
            output_in,
            hidden_grad,
            dec_in[:quarter],
            dec_mod,
            all_live,
            dec_attn_saved,
            dec_attn,
            core,
        )
        parts, dec_feed_sum = tie(parts, dec_feed_sum)
        dec_grad, dec_low, mods_a = modulate_back(
            parts,
            dec_in[:quarter],
            hidden_grad,
            jnp.broadcast_to(uncovered[:quarter, None], hidden_grad.shape),
            dec_mod[1][None],
            ones,
        )
        mask_part = mods_a[2]
        dec_mods = (mods_a[0:2], mods_b[2:3], mods_b[0:2])
        dec_low = gather_rows(dec_low)

    with jax.named_scope("encoder_back"):
        enc_cot = mm(place, dec_low)
        down_in = (enc_mod[5][None] * enc_cot).astype(BF)
        act_grad = mm(down_in, enc_feed[:, feed_width:])
        up_grad = jax.vjp(gelu_tanh, enc_up_value)[1](act_grad)[0].astype(BF)
        partial = mm_nt(up_grad, enc_feed[:, :feed_width], BF)
        partial, dec_act = tie(partial, dec_act)
        (hidden_grad, output_in, mods_b), enc_feed_sum = block_back_feed(
            up_grad,
            partial,
            down_in,
            enc_act,
            enc_cot[:quarter],
            enc_mod,
            enc_feed_saved,
            core,
            True,
        )
        output_in, dec_attn_sum = tie(output_in, dec_attn_sum)
        output_in = gather_rows(output_in)
        branch_b = feed_down(dec_act, dec_feed)
        dec_out = dec_feed_saved[0] + dec_mod[5][None] * branch_b
        gate_grad = jnp.sum(image_cot[:quarter].astype(F32) * branch_b, axis=0, keepdims=True)
        dec_mods = dec_mods + (gate_grad,)
        enc_gate_grad = jnp.sum(enc_cot[:quarter] * enc_branch_b, axis=0, keepdims=True)
        dec_out = gather_rows(dec_out.astype(BF))
        layer_out = both_images(mm_tn(restore, jnp.where(is_first, sent, dec_out), BF))
        parts, enc_attn_sum = block_back_attention(
            output_in,
            hidden_grad,
            enc_in[:quarter],
            enc_mod,
            live,
            enc_attn_saved,
            enc_attn,
            core,
        )
        parts, enc_feed_sum, layer_out = tie(parts, enc_feed_sum, layer_out)
        _, enc_low, mods_a = modulate_back(
            parts, enc_in[:quarter], hidden_grad, hidden_grad, enc_mod[1][None], ones
        )
        enc_low = gather_rows(enc_low)
        enc_mods = (mods_a[0:2], mods_b[2:3], mods_b[0:2], enc_gate_grad)

    with jax.named_scope("modulation_back"):
        mod_parts = jnp.concatenate(enc_mods + dec_mods, axis=0)
        mod_parts = lax.all_to_all(mod_parts.reshape(8, -1), PLANE, 0, 0, tiled=True)
        mod_parts, enc_feed_sum, enc_low = tie(mod_parts, enc_feed_sum, enc_low)
        mod_grad = planes_gather(jnp.sum(mod_parts.reshape(4, 2, -1), axis=0))

    with jax.named_scope("outputs"):
        arrange = jnp.where(is_first, place_plain, restore)
        in_grads = both_images(mm_tn(arrange, jnp.where(is_first, enc_low, dec_low), BF))

    with jax.named_scope("returns"):
        keep, given = return_over_section(enc_feed_sum, dec_feed_sum, section)

    with jax.named_scope("modulation_back"):
        grad_adaln = lax.dot_general(
            cond_rows.astype(F32), mod_grad, (((0,), (0,)), ((), ())), precision=PRECISE
        )

    with jax.named_scope("norm"):
        square = jnp.sum(grad_adaln * grad_adaln)
        for part in (dec_attn_sum, dec_feed_sum, enc_feed_sum):
            square = square + squared(part)
        square, grad_adaln, keep, given, in_grads, dec_attn_sum, enc_attn_sum = tie(
            square, grad_adaln, keep, given, in_grads, dec_attn_sum, enc_attn_sum
        )
        feed_grad = return_over_core(keep, given, section, core)
        down_grad = turned(feed_grad[:, feed_width:])
        up_grad = feed_grad[:, :feed_width]
        square = square + squared(enc_attn_sum)
        totals = jnp.concatenate([mask_part, jnp.full((128,), square / 128.0, F32)])
        totals = sum_over(totals.reshape(1, -1), ("dp",))
        keep, given = return_over_section(enc_attn_sum, dec_attn_sum, section)
        totals, keep, given = tie(totals, keep, given)
        totals = sum_over(totals, ("row", "section", "core"))[0]
        attn_grad = return_over_core(keep, given, section, core)
        heads_grad = jnp.stack([attn_grad[:, i * columns : (i + 1) * columns] for i in range(3)])
        output_grad = turned(attn_grad[:, 3 * columns :])
        totals, heads_grad, output_grad, up_grad, down_grad = tie(
            totals, heads_grad, output_grad, up_grad, down_grad
        )
        mask_total = totals[:model_width]
        grad_norm = jnp.sqrt(jnp.sum(totals[model_width:]) + jnp.sum(mask_total * mask_total))
        factor = jnp.minimum(1.0, CLIP_NORM / (grad_norm + NORM_EPS))

    with jax.named_scope("update"):
        gradients = [
            part.astype(F32)[None] for part in (heads_grad, output_grad, up_grad, down_grad)
        ] + [grad_adaln[None]]
        masters = (heads_weight, output_weight, up_weight, down_weight, adaln_weight)
        firsts = (heads_first, output_first, up_first, down_first, adaln_first)
        seconds = (heads_second, output_second, up_second, down_second, adaln_second)
        updated = []
        for position in range(5):
            updated += adam_update(
                masters[position], firsts[position], seconds[position], gradients[position], factor
            )
        mask_next = adam_update(mask_token, mask_first, mask_second, mask_total, factor)

    return (layer_out, in_grads, *updated, *mask_next, grad_norm)


def solution(mesh):
    sizes = dict(mesh.shape)
    parted = Mesh(
        mesh.devices.reshape(sizes["section"], sizes["tensor"] // 2, 2, sizes["dp"]),
        ("section", "row", "core", "dp"),
    )
    tensor = ("row", "core")
    heads = P("section", None, "dp", tensor)
    tensor_dp = P("section", tensor, "dp")
    dp_tensor = P("section", "dp", tensor)
    weights = [heads] * 3 + [tensor_dp] * 3 + [dp_tensor] * 3 + [tensor_dp] * 3 + [dp_tensor] * 3
    images = P("dp", None, None)
    layers = P("section", "dp", None, None)
    return jax.shard_map(
        per_device,
        mesh=parted,
        in_specs=(
            images,
            images,
            P("dp", None),
            P("dp"),
            P("dp"),
            P("dp"),
            P(),
            *weights,
            P(),
            P(),
            P(),
        ),
        out_specs=(layers, layers, *weights, P(), P(), P(), P()),
        check_vma=False,
    )
```

```python
import math

import jax
import jax.numpy as jnp
from jax import lax
from jax.experimental import pallas as pl
from jax.experimental.pallas import tpu as pltpu
from jax.sharding import Mesh
from jax.sharding import PartitionSpec as P

HEAD_DIM = 72
STEP = 10

PRECISE = lax.Precision.HIGHEST
NORM_EPS = 1e-06
BETA_ONE = 0.9
BETA_TWO = 0.99
LEARN_RATE = 0.05
WEIGHT_DECAY = 0.01
ADAM_EPS = 1e-08
CLIP_NORM = 1.0
MASK_SCORE = -1000000000.0

BF = jnp.bfloat16
F32 = jnp.float32
PLANE = ("section", "row", "core")
CHIPS = ("section", "row")
ROWS_BY = ("dp", "core")


def dot(left, right, dims, out=F32):
    return lax.dot_general(left, right, (dims, ((), ())), preferred_element_type=F32).astype(out)


def mm(left, right, out=F32):
    return dot(left, right, ((1,), (0,)), out)


def mm_nt(left, right, out=F32):
    return dot(left, right, ((1,), (1,)), out)


def mm_tn(left, right, out=F32):
    return dot(left, right, ((0,), (0,)), out)


def turned(values):
    return mm_tn(values, jnp.eye(values.shape[0], dtype=values.dtype), values.dtype)


def chip_route(offset):
    return [
        (s * 2 + r, (s ^ (offset & 1)) * 2 + (r ^ (offset >> 1)))
        for s in range(2)
        for r in range(2)
    ]


def swap_chips(block, offset):
    return lax.ppermute(block, CHIPS, chip_route(offset))


def swap_cores(block):
    return lax.ppermute(block, "core", [(0, 1), (1, 0)])


def gather_rows(own):
    return jnp.concatenate([own] + [swap_chips(own, offset) for offset in (1, 2, 3)], axis=0)


def spread_rows(partial):
    count = partial.shape[0] // 4
    parts = [
        swap_chips(partial[offset * count : (offset + 1) * count], offset) for offset in (3, 2, 1)
    ]
    return [partial[:count]] + parts


def sum_rows(partial):
    return sum(part.astype(F32) for part in spread_rows(partial))


def xor_route(size, offset):
    return [(i, i ^ offset) for i in range(size)]


def planes_gather(block):
    size = lax.axis_size("dp")
    parts = [block] + [
        lax.ppermute(block, "dp", xor_route(size, offset)) for offset in range(1, size)
    ]
    return jnp.concatenate(parts, axis=0)


def planes_sum(blocks):
    size = lax.axis_size("dp")
    count = blocks.shape[0] // size
    total = blocks[:count]
    for offset in range(1, size):
        part = blocks[offset * count : (offset + 1) * count]
        total = total + lax.ppermute(part, "dp", xor_route(size, offset))
    return total


def sum_over(values, axes):
    for axis in axes:
        size = lax.axis_size(axis)
        step = 1
        while step < size:
            values = values + lax.ppermute(values, axis, xor_route(size, step))
            step *= 2
    return values


def send_shares(pack, section, core):
    half = pack.shape[0] // 2
    mine = lax.dynamic_slice_in_dim(pack, core * half, half, 0)
    other = swap_cores(lax.dynamic_slice_in_dim(pack, (1 - core) * half, half, 0))
    keep = jnp.where(core == section, mine, other)
    give = jnp.where(core == section, other, mine)
    return keep, lax.ppermute(give, "section", [(0, 1), (1, 0)])


def by_block(keep, given, section):
    return (jnp.where(section == 0, keep, given), jnp.where(section == 0, given, keep))


def assemble_kernel(order_ref, mine_ref, other_ref, out_ref):
    count = mine_ref.shape[1]
    for part in range(4):
        for which, source in enumerate((mine_ref, other_ref)):
            start = pl.multiple_of(order_ref[which * 4 + part] * count, count)
            out_ref[pl.ds(start, count), :] = source[part]


def assemble(parts, plane, core):
    mine = jnp.stack(parts)
    other = swap_cores(mine)
    planes = jnp.stack([plane ^ offset for offset in range(4)]).astype(jnp.int32)
    order = jnp.concatenate([planes * 2 + core, planes * 2 + 1 - core])
    whole = pl.BlockSpec(memory_space=pltpu.VMEM)
    return pl.pallas_call(
        assemble_kernel,
        out_shape=jax.ShapeDtypeStruct((8 * mine.shape[1], mine.shape[2]), mine.dtype),
        in_specs=[pl.BlockSpec(memory_space=pltpu.SMEM), whole, whole],
        out_specs=whole,
        compiler_params=pltpu.CompilerParams(vmem_limit_bytes=24 * 2**20),
        cost_estimate=pl.CostEstimate(
            flops=0, bytes_accessed=8 * mine.size, transcendentals=0
        ),
    )(order, mine, other)


def return_over_section(first, second, section):
    keep = jnp.where(section == 0, first, second)
    give = jnp.where(section == 0, second, first)
    return (keep, lax.ppermute(give, "section", [(0, 1), (1, 0)]))


def return_over_core(keep, given, section, core):
    mine = jnp.where(core == section, keep, given)
    other = swap_cores(jnp.where(core == section, given, keep))
    top = jnp.where(core == 0, mine, other)
    bottom = jnp.where(core == 0, other, mine)
    return jnp.concatenate([top, bottom], axis=0)


def tie(*values):
    return lax.optimization_barrier(values)


def gather_weight(half):
    return lax.all_gather(half, ROWS_BY, axis=0, tiled=True)


def sum_cores(core, *grads):
    planes = lax.axis_size("dp")
    sums = []
    for grad in grads:
        halves = grad.reshape(planes, 2, grad.shape[0] // planes // 2, grad.shape[1])
        theirs = swap_cores(lax.dynamic_index_in_dim(halves, 1 - core, 1, keepdims=False))
        mine = lax.dynamic_index_in_dim(halves, core, 1, keepdims=False)
        sums.append((mine.astype(F32) + theirs.astype(F32)).astype(BF))
    return jnp.concatenate(sums, axis=2)


def sum_planes(grad):
    summed = lax.psum_scatter(grad, "dp", scatter_dimension=0, tiled=True)
    return summed.reshape(summed.shape[1:])


def normalize(values):
    center = values - jnp.mean(values, axis=-1, keepdims=True)
    spread = jnp.mean(center * center, axis=-1, keepdims=True)
    scale = lax.rsqrt(spread + NORM_EPS)
    return (center * scale, scale)


def modulate(values, shift, scale):
    return normalize(values)[0] * (1.0 + scale) + shift


def modulate_back_kernel(
    own, first, second, third, values_ref, residual, branch, scale, gate, grad_out, low_out, sums_out
):
    grad = own[...].astype(F32) + first[...].astype(F32)
    grad = grad + second[...].astype(F32) + third[...].astype(F32)
    unit, inverse = normalize(values_ref[...])
    inner = grad * (1.0 + scale[...])
    mean_one = jnp.mean(inner, axis=-1, keepdims=True)
    mean_two = jnp.mean(inner * unit, axis=-1, keepdims=True)
    result = (inner - mean_one - unit * mean_two) * inverse + residual[...]
    grad_out[...] = result
    low_out[...] = (result * gate[...]).astype(BF)
    sums_out[0:1, :] = jnp.sum(grad, axis=0, keepdims=True)
    sums_out[1:2, :] = jnp.sum(grad * unit, axis=0, keepdims=True)
    sums_out[2:3, :] = jnp.sum(result * branch[...], axis=0, keepdims=True)


def modulate_back(parts, values, residual, branch, scale, gate):
    rows, width = values.shape
    whole = pl.BlockSpec(memory_space=pltpu.VMEM)
    return pl.pallas_call(
        modulate_back_kernel,
        out_shape=(
            jax.ShapeDtypeStruct((rows, width), F32),
            jax.ShapeDtypeStruct((rows, width), BF),
            jax.ShapeDtypeStruct((8, width), F32),
        ),
        in_specs=[whole] * 9,
        out_specs=(whole, whole, whole),
        compiler_params=pltpu.CompilerParams(vmem_limit_bytes=16 * 2**20),
        cost_estimate=pl.CostEstimate(
            flops=30 * rows * width, bytes_accessed=26 * rows * width, transcendentals=rows
        ),
    )(*parts, values, residual, branch, scale, gate)


def feed_both_kernel(normed, up_ref, down_ref, down_in, act_out, grad_out, part_out, total):
    step = pl.program_id(0)
    up_value = jnp.dot(normed[...], up_ref[...], preferred_element_type=F32)
    inner = math.sqrt(2.0 / math.pi) * (up_value + 0.044715 * up_value * up_value * up_value)
    bend = jnp.tanh(inner)
    act_out[...] = (0.5 * up_value * (1.0 + bend)).astype(BF)
    slope = math.sqrt(2.0 / math.pi) * (1.0 + 3 * 0.044715 * up_value * up_value)
    slope = 0.5 * (1.0 + bend) + 0.5 * up_value * (1.0 - bend * bend) * slope
    act_grad = jnp.dot(down_in[...], down_ref[...], preferred_element_type=F32)
    up_grad = (slope * act_grad).astype(BF)
    grad_out[...] = up_grad
    part = mm_nt(up_grad, up_ref[...])

    @pl.when(step == 0)
    def _():
        total[...] = part

    @pl.when(step > 0)
    def _():
        total[...] += part

    @pl.when(step == pl.num_programs(0) - 1)
    def _():
        part_out[...] = total[...].astype(BF)


def feed_both(normed, feed, down_in):
    rows, width = normed.shape
    units = feed.shape[1] // 2
    tile = units // 3
    return pl.pallas_call(
        feed_both_kernel,
        grid=(3,),
        out_shape=(
            jax.ShapeDtypeStruct((rows, units), BF),
            jax.ShapeDtypeStruct((rows, units), BF),
            jax.ShapeDtypeStruct((rows, width), BF),
        ),
        in_specs=[
            pl.BlockSpec((rows, width), lambda j: (0, 0)),
            pl.BlockSpec((width, tile), lambda j: (0, j)),
            pl.BlockSpec((width, tile), lambda j: (0, j + 3)),
            pl.BlockSpec((rows, width), lambda j: (0, 0)),
        ],
        out_specs=(
            pl.BlockSpec((rows, tile), lambda j: (0, j)),
            pl.BlockSpec((rows, tile), lambda j: (0, j)),
            pl.BlockSpec((rows, width), lambda j: (0, 0)),
        ),
        scratch_shapes=[pltpu.VMEM((rows, width), F32)],
        compiler_params=pltpu.CompilerParams(
            dimension_semantics=("arbitrary",), vmem_limit_bytes=32 * 2**20
        ),
        cost_estimate=pl.CostEstimate(
            flops=6 * rows * width * units,
            bytes_accessed=4 * width * units + 10 * rows * width,
            transcendentals=rows * units,
        ),
    )(normed, feed, feed, down_in)


def gelu_tanh(values):
    return jax.nn.gelu(values, approximate=True)


def time_embed(steps_in, model_width):
    half_width = model_width // 2
    frequency = jnp.exp(-math.log(10000.0) * jnp.arange(half_width, dtype=F32) / half_width)
    angles = steps_in.astype(F32)[:, None] * frequency[None, :]
    return jnp.concatenate([jnp.cos(angles), jnp.sin(angles)], axis=-1)


def split_heads(stacked):
    rows, width = stacked.shape
    parts = stacked.reshape(rows, 3, width // 3 // HEAD_DIM, HEAD_DIM)
    return parts[:, 0], parts[:, 1], parts[:, 2]


def scores_of(queries, keys_in, live):
    scores = jnp.einsum("qhe,khe->hqk", queries, keys_in, preferred_element_type=F32)
    return jnp.where(live[None, None, :] > 0, scores * HEAD_DIM ** (-0.5), MASK_SCORE)


def attend(stacked, live):
    queries, keys_in, values = split_heads(stacked)
    scores = scores_of(queries, keys_in, live)
    row_peak = jnp.max(scores, axis=-1, keepdims=True)
    exponent = jnp.exp(scores - row_peak)
    row_total = jnp.sum(exponent, axis=-1, keepdims=True)
    probability = (exponent / row_total).astype(BF)
    attended = jnp.einsum("hqk,khe->qhe", probability, values, preferred_element_type=F32)
    return attended.astype(BF).reshape(stacked.shape[0], -1), row_peak + jnp.log(row_total)


def attend_back(attended_grad, stacked, live, log_total):
    rows = stacked.shape[0]
    queries, keys_in, values = split_heads(stacked)
    grad = attended_grad.reshape(values.shape)
    soft = jnp.exp(scores_of(queries, keys_in, live) - log_total)
    value_grad = jnp.einsum("hqk,qhe->khe", soft.astype(BF), grad, preferred_element_type=F32)
    prob_grad = jnp.einsum("qhe,khe->hqk", grad, values, preferred_element_type=F32)
    score_grad = soft * (prob_grad - jnp.sum(soft * prob_grad, axis=-1, keepdims=True))
    score_grad = score_grad.astype(BF)
    scale = HEAD_DIM ** (-0.5)
    query_grad = jnp.einsum("hqk,khe->qhe", score_grad, keys_in, preferred_element_type=F32) * scale
    key_grad = jnp.einsum("hqk,qhe->khe", score_grad, queries, preferred_element_type=F32) * scale
    stacked_grad = jnp.stack([query_grad, key_grad, value_grad], axis=1).astype(BF)
    return stacked_grad.reshape(rows, -1)


def block_attention(inputs, mod, live, w_attn, own_count):
    columns = w_attn.shape[1] // 4
    shift_a, scale_a, gate_a, shift_b, scale_b = (mod[i][None] for i in range(5))
    normed = modulate(inputs, shift_a, scale_a).astype(BF)
    stacked = mm(normed, w_attn[:, : 3 * columns], BF)
    attended, log_total = attend(stacked, live)
    branch_a = sum_rows(mm_nt(attended, w_attn[:, 3 * columns :], BF))
    hidden = inputs[:own_count] + gate_a * branch_a
    normed_b = gather_rows(modulate(hidden, shift_b, scale_b).astype(BF))
    padded = jnp.pad(attended, ((0, 0), (3 * columns, 0)))
    normed_b, padded = tie(normed_b, padded)
    return (normed, stacked, padded, log_total, branch_a, hidden, normed_b)


def block_back_feed(up_grad, partial, down_in, activated, grad_own, mod, saved, core, late):
    hidden, normed_b, branch_a = saved
    partial, up_grad, down_in, activated = tie(partial, up_grad, down_in, activated)
    grad_down = mm_tn(down_in, activated, BF)
    grad_up = mm_tn(normed_b, up_grad, BF)
    grads = sum_cores(core, grad_up, grad_down)
    if late:
        parts, grads = tie(spread_rows(partial), grads)
    else:
        partial, grads = tie(partial, grads)
        parts = spread_rows(partial)
    feed_sum = sum_planes(grads)
    return modulate_back(parts, hidden, grad_own, branch_a, mod[4][None], mod[2][None]), feed_sum


def block_back_attention(output_in, hidden_grad, inputs_own, mod, live, saved, w_attn, core):
    normed, stacked, padded, log_total = saved
    columns = w_attn.shape[1] // 4
    attended_grad = mm(output_in, w_attn[:, 3 * columns :], BF)
    stacked_grad = attend_back(attended_grad, stacked, live, log_total)
    partial = mm_nt(stacked_grad, w_attn[:, : 3 * columns], BF)
    partial, stacked_grad, output_in = tie(partial, stacked_grad, output_in)
    lefts = jnp.concatenate([normed, output_in], axis=0)
    wide_grad = jnp.pad(stacked_grad, ((0, 0), (0, columns)))
    grad_attn = mm_tn(lefts, jnp.concatenate([wide_grad, padded], axis=0), BF)
    parts, grad_attn = tie(spread_rows(partial), sum_cores(core, grad_attn))
    attn_sum = sum_planes(grad_attn)
    return parts, attn_sum


def squared(values):
    wide = values.astype(F32)
    return jnp.sum(wide * wide)


def adam_update(weight_in, first_in, second_in, gradient, factor):
    clipped = gradient * factor
    first_out = BETA_ONE * first_in + (1.0 - BETA_ONE) * clipped
    second_out = BETA_TWO * second_in + (1.0 - BETA_TWO) * clipped * clipped
    ratio = (
        first_out
        / (1.0 - BETA_ONE**STEP)
        / (jnp.sqrt(second_out / (1.0 - BETA_TWO**STEP)) + ADAM_EPS)
    )
    weight_out = weight_in - LEARN_RATE * (ratio + WEIGHT_DECAY * weight_in)
    return (weight_out, first_out, second_out)


def per_device(
    tokens,
    cotangent,
    kept_index,
    full_flag,
    labels,
    timesteps,
    class_table,
    heads_weight,
    heads_first,
    heads_second,
    output_weight,
    output_first,
    output_second,
    up_weight,
    up_first,
    up_second,
    down_weight,
    down_first,
    down_second,
    adaln_weight,
    adaln_first,
    adaln_second,
    mask_token,
    mask_first,
    mask_second,
):
    image_count, seq_length, model_width = tokens.shape
    section = lax.axis_index("section")
    core = lax.axis_index("core")
    plane = lax.axis_index("dp")
    chip = lax.axis_index("row") * 2 + section
    quarter = seq_length // 4
    shard = model_width // lax.axis_size("dp")
    columns = heads_weight.shape[-1]

    with jax.named_scope("weights_in"):
        attn_pack = jnp.concatenate(
            [heads_weight[0, 0], heads_weight[0, 1], heads_weight[0, 2], output_weight[0].T], axis=1
        ).astype(BF)
        keep, given = send_shares(attn_pack, section, core)
        attn_width = attn_pack.shape[1]
        if lax.axis_size("dp") == 4:
            cut = attn_width // 3
            first = keep[:, :cut]
            parts = [first] + [lax.ppermute(first, "dp", xor_route(4, m)) for m in (1, 2, 3)]
            given, *parts = tie(given, *parts)
            rest = gather_weight(jnp.concatenate([given, keep[:, cut:]], axis=1))
            keep_all = jnp.concatenate([assemble(parts, plane, core), rest[:, attn_width:]], axis=1)
        else:
            rest = gather_weight(jnp.concatenate([given, keep], axis=1))
            keep_all = rest[:, attn_width:]
        enc_attn, dec_attn = by_block(keep_all, rest[:, :attn_width], section)
        feed_pack = jnp.concatenate([up_weight[0], down_weight[0].T], axis=1).astype(BF)
        feed_pack, given = tie(feed_pack, given)
        enc_feed_half, dec_feed_half = by_block(*send_shares(feed_pack, section, core), section)
        feed_width = feed_pack.shape[1] // 2
        enc_feed = gather_weight(enc_feed_half)

    with jax.named_scope("modulation"):
        codes = planes_gather(jnp.stack([labels, timesteps], axis=1))
        class_count = class_table.shape[0]
        label_hot = (codes[:, :1] == jnp.arange(class_count, dtype=jnp.int32)[None, :]).astype(BF)
        condition = mm(label_hot, class_table) + time_embed(codes[:, 1], model_width)
        cond_act = jax.nn.silu(condition).astype(BF)
        cond_rows = lax.dynamic_slice_in_dim(cond_act, plane * shard, shard, 1)
        adaln_part = planes_sum(mm(cond_rows, adaln_weight[0].astype(BF)))
        adaln_all = lax.all_gather(adaln_part, PLANE, axis=0, tiled=False)
        mod_all = lax.dynamic_index_in_dim(adaln_all, core, 1, keepdims=False)
        mod_all = mod_all.reshape(2, 6, model_width)
        enc_mod, dec_mod = mod_all[0], mod_all[1]

    def relative(values):
        parts = [
            lax.dynamic_slice_in_dim(values, (chip ^ offset) * quarter, quarter, 0)
            for offset in range(4)
        ]
        return jnp.concatenate(parts, axis=0)

    with jax.named_scope("placement"):
        image_tokens = lax.dynamic_index_in_dim(tokens, core, 0, keepdims=False)
        image_cot = relative(lax.dynamic_index_in_dim(cotangent, core, 0, keepdims=False))
        kept = relative(lax.dynamic_index_in_dim(kept_index, core, 0, keepdims=False))
        flag = lax.dynamic_index_in_dim(full_flag, core, 0, keepdims=False)
        plain_ids = jnp.arange(seq_length, dtype=jnp.int32)
        ids = ((plain_ids // quarter) ^ chip) * quarter + plain_ids % quarter
        live = ids < jnp.where(flag > 0, seq_length, seq_length // 2)
        place_plain = ((kept[:, None] == plain_ids[None, :]) & live[:, None]).astype(BF)
        place = ((kept[:, None] == ids[None, :]) & live[:, None]).astype(BF)
        live = live.astype(F32)
        uncovered = 1.0 - jnp.sum(place.astype(F32), axis=0)
        restore = (ids[:, None] == plain_ids[None, :]).astype(BF)
        enc_in = mm(place_plain, image_tokens)

    def feed_up(normed_b, feed):
        up_value = mm(normed_b, feed[:, :feed_width])
        return up_value, gelu_tanh(up_value).astype(BF)

    def feed_down(activated, feed):
        return sum_rows(mm_nt(activated, feed[:, feed_width:], BF))

    with jax.named_scope("encoder"):
        normed, stacked, attended, log_total, branch_a, hidden, normed_b = block_attention(
            enc_in, enc_mod, live, enc_attn, quarter
        )
        normed_b, dec_feed_half = tie(normed_b, dec_feed_half)
        dec_feed = gather_weight(dec_feed_half)
        enc_up_value, enc_act = feed_up(normed_b, enc_feed)
        branch_b = feed_down(enc_act, enc_feed)
        enc_branch_b = branch_b
        enc_out = (hidden + enc_mod[5][None] * branch_b) * live[:quarter, None]
        sent = gather_rows(enc_out.astype(BF))
        enc_attn_saved = (normed, stacked, attended, log_total)
        enc_feed_saved = (hidden, normed_b, branch_a)

    with jax.named_scope("decoder"):
        dec_in = mm_tn(place, sent) + uncovered[:, None] * mask_token[None, :]
        all_live = jnp.ones_like(live)
        normed, stacked, attended, log_total, branch_a, hidden, normed_b = block_attention(
            dec_in, dec_mod, all_live, dec_attn, quarter
        )
        dec_down_in = (dec_mod[5][None] * image_cot.astype(F32)).astype(BF)
        dec_act, dec_up_grad, dec_partial = feed_both(normed_b, dec_feed, dec_down_in)
        dec_attn_saved = (normed, stacked, attended, log_total)
        dec_feed_saved = (hidden, normed_b, branch_a)

    is_first = section == 0

    def both_images(mine):
        other = swap_cores(mine)
        pair = jnp.where(core == 0, jnp.stack([mine, other]), jnp.stack([other, mine]))
        return pair[None]

    ones = jnp.ones((1, model_width), F32)

    with jax.named_scope("decoder_back"):
        (hidden_grad, output_in, mods_b), dec_feed_sum = block_back_feed(
            dec_up_grad,
            dec_partial,
            dec_down_in,
            dec_act,
            image_cot[:quarter].astype(F32),
            dec_mod,
            dec_feed_saved,
            core,
            False,
        )
        output_in = gather_rows(output_in)
        parts, dec_attn_sum = block_back_attention(
            output_in,
            hidden_grad,
            dec_in[:quarter],
            dec_mod,
            all_live,
            dec_attn_saved,
            dec_attn,
            core,
        )
        parts, dec_feed_sum = tie(parts, dec_feed_sum)
        dec_grad, dec_low, mods_a = modulate_back(
            parts,
            dec_in[:quarter],
            hidden_grad,
            jnp.broadcast_to(uncovered[:quarter, None], hidden_grad.shape),
            dec_mod[1][None],
            ones,
        )
        mask_part = mods_a[2]
        dec_mods = (mods_a[0:2], mods_b[2:3], mods_b[0:2])
        dec_low = gather_rows(dec_low)

    with jax.named_scope("encoder_back"):
        enc_cot = mm(place, dec_low)
        down_in = (enc_mod[5][None] * enc_cot).astype(BF)
        act_grad = mm(down_in, enc_feed[:, feed_width:])
        up_grad = jax.vjp(gelu_tanh, enc_up_value)[1](act_grad)[0].astype(BF)
        partial = mm_nt(up_grad, enc_feed[:, :feed_width], BF)
        partial, dec_act = tie(partial, dec_act)
        (hidden_grad, output_in, mods_b), enc_feed_sum = block_back_feed(
            up_grad,
            partial,
            down_in,
            enc_act,
            enc_cot[:quarter],
            enc_mod,
            enc_feed_saved,
            core,
            True,
        )
        output_in, dec_attn_sum = tie(output_in, dec_attn_sum)
        output_in = gather_rows(output_in)
        branch_b = feed_down(dec_act, dec_feed)
        dec_out = dec_feed_saved[0] + dec_mod[5][None] * branch_b
        gate_grad = jnp.sum(image_cot[:quarter].astype(F32) * branch_b, axis=0, keepdims=True)
        dec_mods = dec_mods + (gate_grad,)
        enc_gate_grad = jnp.sum(enc_cot[:quarter] * enc_branch_b, axis=0, keepdims=True)
        dec_out = gather_rows(dec_out.astype(BF))
        layer_out = both_images(mm_tn(restore, jnp.where(is_first, sent, dec_out), BF))
        parts, enc_attn_sum = block_back_attention(
            output_in,
            hidden_grad,
            enc_in[:quarter],
            enc_mod,
            live,
            enc_attn_saved,
            enc_attn,
            core,
        )
        parts, enc_feed_sum, layer_out = tie(parts, enc_feed_sum, layer_out)
        _, enc_low, mods_a = modulate_back(
            parts, enc_in[:quarter], hidden_grad, hidden_grad, enc_mod[1][None], ones
        )
        enc_low = gather_rows(enc_low)
        enc_mods = (mods_a[0:2], mods_b[2:3], mods_b[0:2], enc_gate_grad)

    with jax.named_scope("modulation_back"):
        mod_parts = jnp.concatenate(enc_mods + dec_mods, axis=0)
        mod_parts = lax.all_to_all(mod_parts.reshape(8, -1), PLANE, 0, 0, tiled=True)
        mod_parts, enc_feed_sum, enc_low = tie(mod_parts, enc_feed_sum, enc_low)
        mod_grad = planes_gather(jnp.sum(mod_parts.reshape(4, 2, -1), axis=0))

    with jax.named_scope("outputs"):
        arrange = jnp.where(is_first, place_plain, restore)
        in_grads = both_images(mm_tn(arrange, jnp.where(is_first, enc_low, dec_low), BF))

    with jax.named_scope("returns"):
        keep, given = return_over_section(enc_feed_sum, dec_feed_sum, section)

    with jax.named_scope("modulation_back"):
        grad_adaln = lax.dot_general(
            cond_rows.astype(F32), mod_grad, (((0,), (0,)), ((), ())), precision=PRECISE
        )

    with jax.named_scope("norm"):
        square = jnp.sum(grad_adaln * grad_adaln)
        for part in (dec_attn_sum, dec_feed_sum, enc_feed_sum):
            square = square + squared(part)
        square, grad_adaln, keep, given, in_grads, dec_attn_sum, enc_attn_sum = tie(
            square, grad_adaln, keep, given, in_grads, dec_attn_sum, enc_attn_sum
        )
        feed_grad = return_over_core(keep, given, section, core)
        down_grad = turned(feed_grad[:, feed_width:])
        up_grad = feed_grad[:, :feed_width]
        square = square + squared(enc_attn_sum)
        totals = jnp.concatenate([mask_part, jnp.full((128,), square / 128.0, F32)])
        totals = sum_over(totals.reshape(1, -1), ("dp",))
        keep, given = return_over_section(enc_attn_sum, dec_attn_sum, section)
        totals, keep, given = tie(totals, keep, given)
        totals = sum_over(totals, ("row", "section", "core"))[0]
        attn_grad = return_over_core(keep, given, section, core)
        heads_grad = jnp.stack([attn_grad[:, i * columns : (i + 1) * columns] for i in range(3)])
        output_grad = turned(attn_grad[:, 3 * columns :])
        totals, heads_grad, output_grad, up_grad, down_grad = tie(
            totals, heads_grad, output_grad, up_grad, down_grad
        )
        mask_total = totals[:model_width]
        grad_norm = jnp.sqrt(jnp.sum(totals[model_width:]) + jnp.sum(mask_total * mask_total))
        factor = jnp.minimum(1.0, CLIP_NORM / (grad_norm + NORM_EPS))

    with jax.named_scope("update"):
        gradients = [
            part.astype(F32)[None] for part in (heads_grad, output_grad, up_grad, down_grad)
        ] + [grad_adaln[None]]
        masters = (heads_weight, output_weight, up_weight, down_weight, adaln_weight)
        firsts = (heads_first, output_first, up_first, down_first, adaln_first)
        seconds = (heads_second, output_second, up_second, down_second, adaln_second)
        updated = []
        for position in range(5):
            updated += adam_update(
                masters[position], firsts[position], seconds[position], gradients[position], factor
            )
        mask_next = adam_update(mask_token, mask_first, mask_second, mask_total, factor)

    return (layer_out, in_grads, *updated, *mask_next, grad_norm)


def solution(mesh):
    sizes = dict(mesh.shape)
    parted = Mesh(
        mesh.devices.reshape(sizes["section"], sizes["tensor"] // 2, 2, sizes["dp"]),
        ("section", "row", "core", "dp"),
    )
    tensor = ("row", "core")
    heads = P("section", None, "dp", tensor)
    tensor_dp = P("section", tensor, "dp")
    dp_tensor = P("section", "dp", tensor)
    weights = [heads] * 3 + [tensor_dp] * 3 + [dp_tensor] * 3 + [tensor_dp] * 3 + [dp_tensor] * 3
    images = P("dp", None, None)
    layers = P("section", "dp", None, None)
    return jax.shard_map(
        per_device,
        mesh=parted,
        in_specs=(
            images,
            images,
            P("dp", None),
            P("dp"),
            P("dp"),
            P("dp"),
            P(),
            *weights,
            P(),
            P(),
            P(),
        ),
        out_specs=(layers, layers, *weights, P(), P(), P(), P()),
        check_vma=False,
    )
```

```python
import math

import jax
import jax.numpy as jnp
from jax import lax
from jax.experimental import pallas as pl
from jax.experimental.pallas import tpu as pltpu
from jax.sharding import Mesh
from jax.sharding import PartitionSpec as P

HEAD_DIM = 72
STEP = 10

PRECISE = lax.Precision.HIGHEST
NORM_EPS = 1e-06
BETA_ONE = 0.9
BETA_TWO = 0.99
LEARN_RATE = 0.05
WEIGHT_DECAY = 0.01
ADAM_EPS = 1e-08
CLIP_NORM = 1.0
MASK_SCORE = -1000000000.0

BF = jnp.bfloat16
F32 = jnp.float32
PLANE = ("section", "row", "core")
CHIPS = ("section", "row")
ROWS_BY = ("dp", "core")


def dot(left, right, dims, out=F32):
    return lax.dot_general(left, right, (dims, ((), ())), preferred_element_type=F32).astype(out)


def mm(left, right, out=F32):
    return dot(left, right, ((1,), (0,)), out)


def mm_nt(left, right, out=F32):
    return dot(left, right, ((1,), (1,)), out)


def mm_tn(left, right, out=F32):
    return dot(left, right, ((0,), (0,)), out)


def turned(values):
    return mm_tn(values, jnp.eye(values.shape[0], dtype=values.dtype), values.dtype)


def chip_route(offset):
    return [
        (s * 2 + r, (s ^ (offset & 1)) * 2 + (r ^ (offset >> 1)))
        for s in range(2)
        for r in range(2)
    ]


def swap_chips(block, offset):
    return lax.ppermute(block, CHIPS, chip_route(offset))


def swap_cores(block):
    return lax.ppermute(block, "core", [(0, 1), (1, 0)])


def gather_rows(own):
    return jnp.concatenate([own] + [swap_chips(own, offset) for offset in (1, 2, 3)], axis=0)


def spread_rows(partial):
    count = partial.shape[0] // 4
    parts = [
        swap_chips(partial[offset * count : (offset + 1) * count], offset) for offset in (3, 2, 1)
    ]
    return [partial[:count]] + parts


def sum_rows(partial):
    return sum(part.astype(F32) for part in spread_rows(partial))


def xor_route(size, offset):
    return [(i, i ^ offset) for i in range(size)]


def planes_gather(block):
    size = lax.axis_size("dp")
    parts = [block] + [
        lax.ppermute(block, "dp", xor_route(size, offset)) for offset in range(1, size)
    ]
    return jnp.concatenate(parts, axis=0)


def planes_sum(blocks):
    size = lax.axis_size("dp")
    count = blocks.shape[0] // size
    total = blocks[:count]
    for offset in range(1, size):
        part = blocks[offset * count : (offset + 1) * count]
        total = total + lax.ppermute(part, "dp", xor_route(size, offset))
    return total


def sum_over(values, axes):
    for axis in axes:
        size = lax.axis_size(axis)
        step = 1
        while step < size:
            values = values + lax.ppermute(values, axis, xor_route(size, step))
            step *= 2
    return values


def send_shares(rows_of, half, section, core):
    other = swap_cores(rows_of((1 - core) * half))
    mine = rows_of(core * half)
    keep = jnp.where(core == section, mine, other)
    give = jnp.where(core == section, other, mine)
    return keep, lax.ppermute(give, "section", [(0, 1), (1, 0)])


def by_block(keep, given, section):
    return (jnp.where(section == 0, keep, given), jnp.where(section == 0, given, keep))


def assemble_kernel(order_ref, mine_ref, other_ref, out_ref):
    count = mine_ref.shape[1]
    for part in range(4):
        for which, source in enumerate((mine_ref, other_ref)):
            start = pl.multiple_of(order_ref[which * 4 + part] * count, count)
            out_ref[pl.ds(start, count), :] = source[part]


def assemble(parts, plane, core):
    mine = jnp.stack(parts)
    other = swap_cores(mine)
    planes = jnp.stack([plane ^ offset for offset in range(4)]).astype(jnp.int32)
    order = jnp.concatenate([planes * 2 + core, planes * 2 + 1 - core])
    whole = pl.BlockSpec(memory_space=pltpu.VMEM)
    return pl.pallas_call(
        assemble_kernel,
        out_shape=jax.ShapeDtypeStruct((8 * mine.shape[1], mine.shape[2]), mine.dtype),
        in_specs=[pl.BlockSpec(memory_space=pltpu.SMEM), whole, whole],
        out_specs=whole,
        compiler_params=pltpu.CompilerParams(vmem_limit_bytes=24 * 2**20),
        cost_estimate=pl.CostEstimate(
            flops=0, bytes_accessed=8 * mine.size, transcendentals=0
        ),
    )(order, mine, other)


def return_over_section(first, second, section):
    keep = jnp.where(section == 0, first, second)
    give = jnp.where(section == 0, second, first)
    return (keep, lax.ppermute(give, "section", [(0, 1), (1, 0)]))


def return_over_core(keep, given, section, core):
    mine = jnp.where(core == section, keep, given)
    other = swap_cores(jnp.where(core == section, given, keep))
    top = jnp.where(core == 0, mine, other)
    bottom = jnp.where(core == 0, other, mine)
    return jnp.concatenate([top, bottom], axis=0)


def tie(*values):
    return lax.optimization_barrier(values)


def gather_weight(half):
    return lax.all_gather(half, ROWS_BY, axis=0, tiled=True)


def sum_cores(core, *grads):
    planes = lax.axis_size("dp")
    sums = []
    for grad in grads:
        halves = grad.reshape(planes, 2, grad.shape[0] // planes // 2, grad.shape[1])
        theirs = swap_cores(lax.dynamic_index_in_dim(halves, 1 - core, 1, keepdims=False))
        mine = lax.dynamic_index_in_dim(halves, core, 1, keepdims=False)
        sums.append((mine.astype(F32) + theirs.astype(F32)).astype(BF))
    return jnp.concatenate(sums, axis=2)


def sum_planes(grad):
    summed = lax.psum_scatter(grad, "dp", scatter_dimension=0, tiled=True)
    return summed.reshape(summed.shape[1:])


def normalize(values):
    center = values - jnp.mean(values, axis=-1, keepdims=True)
    spread = jnp.mean(center * center, axis=-1, keepdims=True)
    scale = lax.rsqrt(spread + NORM_EPS)
    return (center * scale, scale)


def modulate(values, shift, scale):
    return normalize(values)[0] * (1.0 + scale) + shift


def modulate_back_kernel(
    own, first, second, third, values_ref, residual, branch, scale, gate, grad_out, low_out, sums_out
):
    grad = own[...].astype(F32) + first[...].astype(F32)
    grad = grad + second[...].astype(F32) + third[...].astype(F32)
    unit, inverse = normalize(values_ref[...])
    inner = grad * (1.0 + scale[...])
    mean_one = jnp.mean(inner, axis=-1, keepdims=True)
    mean_two = jnp.mean(inner * unit, axis=-1, keepdims=True)
    result = (inner - mean_one - unit * mean_two) * inverse + residual[...]
    grad_out[...] = result
    low_out[...] = (result * gate[...]).astype(BF)
    sums_out[0:1, :] = jnp.sum(grad, axis=0, keepdims=True)
    sums_out[1:2, :] = jnp.sum(grad * unit, axis=0, keepdims=True)
    sums_out[2:3, :] = jnp.sum(result * branch[...], axis=0, keepdims=True)


def modulate_back(parts, values, residual, branch, scale, gate):
    rows, width = values.shape
    whole = pl.BlockSpec(memory_space=pltpu.VMEM)
    return pl.pallas_call(
        modulate_back_kernel,
        out_shape=(
            jax.ShapeDtypeStruct((rows, width), F32),
            jax.ShapeDtypeStruct((rows, width), BF),
            jax.ShapeDtypeStruct((8, width), F32),
        ),
        in_specs=[whole] * 9,
        out_specs=(whole, whole, whole),
        compiler_params=pltpu.CompilerParams(vmem_limit_bytes=16 * 2**20),
        cost_estimate=pl.CostEstimate(
            flops=30 * rows * width, bytes_accessed=26 * rows * width, transcendentals=rows
        ),
    )(*parts, values, residual, branch, scale, gate)


def feed_both_kernel(normed, up_ref, down_ref, down_in, act_out, grad_out, part_out, total):
    step = pl.program_id(0)
    up_value = jnp.dot(normed[...], up_ref[...], preferred_element_type=F32)
    inner = math.sqrt(2.0 / math.pi) * (up_value + 0.044715 * up_value * up_value * up_value)
    bend = jnp.tanh(inner)
    act_out[...] = (0.5 * up_value * (1.0 + bend)).astype(BF)
    slope = math.sqrt(2.0 / math.pi) * (1.0 + 3 * 0.044715 * up_value * up_value)
    slope = 0.5 * (1.0 + bend) + 0.5 * up_value * (1.0 - bend * bend) * slope
    act_grad = jnp.dot(down_in[...], down_ref[...], preferred_element_type=F32)
    up_grad = (slope * act_grad).astype(BF)
    grad_out[...] = up_grad
    part = mm_nt(up_grad, up_ref[...])

    @pl.when(step == 0)
    def _():
        total[...] = part

    @pl.when(step > 0)
    def _():
        total[...] += part

    @pl.when(step == pl.num_programs(0) - 1)
    def _():
        part_out[...] = total[...].astype(BF)


def feed_both(normed, feed, down_in):
    rows, width = normed.shape
    units = feed.shape[1] // 2
    tile = units // 3
    return pl.pallas_call(
        feed_both_kernel,
        grid=(3,),
        out_shape=(
            jax.ShapeDtypeStruct((rows, units), BF),
            jax.ShapeDtypeStruct((rows, units), BF),
            jax.ShapeDtypeStruct((rows, width), BF),
        ),
        in_specs=[
            pl.BlockSpec((rows, width), lambda j: (0, 0)),
            pl.BlockSpec((width, tile), lambda j: (0, j)),
            pl.BlockSpec((width, tile), lambda j: (0, j + 3)),
            pl.BlockSpec((rows, width), lambda j: (0, 0)),
        ],
        out_specs=(
            pl.BlockSpec((rows, tile), lambda j: (0, j)),
            pl.BlockSpec((rows, tile), lambda j: (0, j)),
            pl.BlockSpec((rows, width), lambda j: (0, 0)),
        ),
        scratch_shapes=[pltpu.VMEM((rows, width), F32)],
        compiler_params=pltpu.CompilerParams(
            dimension_semantics=("arbitrary",), vmem_limit_bytes=32 * 2**20
        ),
        cost_estimate=pl.CostEstimate(
            flops=6 * rows * width * units,
            bytes_accessed=4 * width * units + 10 * rows * width,
            transcendentals=rows * units,
        ),
    )(normed, feed, feed, down_in)


def gelu_tanh(values):
    return jax.nn.gelu(values, approximate=True)


def time_embed(steps_in, model_width):
    half_width = model_width // 2
    frequency = jnp.exp(-math.log(10000.0) * jnp.arange(half_width, dtype=F32) / half_width)
    angles = steps_in.astype(F32)[:, None] * frequency[None, :]
    return jnp.concatenate([jnp.cos(angles), jnp.sin(angles)], axis=-1)


def split_heads(stacked):
    rows, width = stacked.shape
    parts = stacked.reshape(rows, 3, width // 3 // HEAD_DIM, HEAD_DIM)
    return parts[:, 0], parts[:, 1], parts[:, 2]


def scores_of(queries, keys_in, live):
    scores = jnp.einsum("qhe,khe->hqk", queries, keys_in, preferred_element_type=F32)
    return jnp.where(live[None, None, :] > 0, scores * HEAD_DIM ** (-0.5), MASK_SCORE)


def attend(stacked, live):
    queries, keys_in, values = split_heads(stacked)
    scores = scores_of(queries, keys_in, live)
    row_peak = jnp.max(scores, axis=-1, keepdims=True)
    exponent = jnp.exp(scores - row_peak)
    row_total = jnp.sum(exponent, axis=-1, keepdims=True)
    probability = (exponent / row_total).astype(BF)
    attended = jnp.einsum("hqk,khe->qhe", probability, values, preferred_element_type=F32)
    return attended.astype(BF).reshape(stacked.shape[0], -1), row_peak + jnp.log(row_total)


def attend_back(attended_grad, stacked, live, log_total):
    rows = stacked.shape[0]
    queries, keys_in, values = split_heads(stacked)
    grad = attended_grad.reshape(values.shape)
    soft = jnp.exp(scores_of(queries, keys_in, live) - log_total)
    value_grad = jnp.einsum("hqk,qhe->khe", soft.astype(BF), grad, preferred_element_type=F32)
    prob_grad = jnp.einsum("qhe,khe->hqk", grad, values, preferred_element_type=F32)
    score_grad = soft * (prob_grad - jnp.sum(soft * prob_grad, axis=-1, keepdims=True))
    score_grad = score_grad.astype(BF)
    scale = HEAD_DIM ** (-0.5)
    query_grad = jnp.einsum("hqk,khe->qhe", score_grad, keys_in, preferred_element_type=F32) * scale
    key_grad = jnp.einsum("hqk,qhe->khe", score_grad, queries, preferred_element_type=F32) * scale
    stacked_grad = jnp.stack([query_grad, key_grad, value_grad], axis=1).astype(BF)
    return stacked_grad.reshape(rows, -1)


def block_attention(inputs, mod, live, w_attn, own_count):
    columns = w_attn.shape[1] // 4
    shift_a, scale_a, gate_a, shift_b, scale_b = (mod[i][None] for i in range(5))
    normed = modulate(inputs, shift_a, scale_a).astype(BF)
    stacked = mm(normed, w_attn[:, : 3 * columns], BF)
    attended, log_total = attend(stacked, live)
    branch_a = sum_rows(mm_nt(attended, w_attn[:, 3 * columns :], BF))
    hidden = inputs[:own_count] + gate_a * branch_a
    normed_b = gather_rows(modulate(hidden, shift_b, scale_b).astype(BF))
    padded = jnp.pad(attended, ((0, 0), (3 * columns, 0)))
    normed_b, padded = tie(normed_b, padded)
    return (normed, stacked, padded, log_total, branch_a, hidden, normed_b)


def block_back_feed(up_grad, partial, down_in, activated, grad_own, mod, saved, core, late):
    hidden, normed_b, branch_a = saved
    partial, up_grad, down_in, activated = tie(partial, up_grad, down_in, activated)
    grad_down = mm_tn(down_in, activated, BF)
    grad_up = mm_tn(normed_b, up_grad, BF)
    grads = sum_cores(core, grad_up, grad_down)
    if late:
        parts, grads = tie(spread_rows(partial), grads)
    else:
        partial, grads = tie(partial, grads)
        parts = spread_rows(partial)
    feed_sum = sum_planes(grads)
    return modulate_back(parts, hidden, grad_own, branch_a, mod[4][None], mod[2][None]), feed_sum


def block_back_attention(output_in, hidden_grad, inputs_own, mod, live, saved, w_attn, core):
    normed, stacked, padded, log_total = saved
    columns = w_attn.shape[1] // 4
    attended_grad = mm(output_in, w_attn[:, 3 * columns :], BF)
    stacked_grad = attend_back(attended_grad, stacked, live, log_total)
    partial = mm_nt(stacked_grad, w_attn[:, : 3 * columns], BF)
    partial, stacked_grad, output_in = tie(partial, stacked_grad, output_in)
    lefts = jnp.concatenate([normed, output_in], axis=0)
    wide_grad = jnp.pad(stacked_grad, ((0, 0), (0, columns)))
    grad_attn = mm_tn(lefts, jnp.concatenate([wide_grad, padded], axis=0), BF)
    parts, grad_attn = tie(spread_rows(partial), sum_cores(core, grad_attn))
    attn_sum = sum_planes(grad_attn)
    return parts, attn_sum


def squared(values):
    wide = values.astype(F32)
    return jnp.sum(wide * wide)


def adam_update(weight_in, first_in, second_in, gradient, factor):
    clipped = gradient * factor
    first_out = BETA_ONE * first_in + (1.0 - BETA_ONE) * clipped
    second_out = BETA_TWO * second_in + (1.0 - BETA_TWO) * clipped * clipped
    ratio = (
        first_out
        / (1.0 - BETA_ONE**STEP)
        / (jnp.sqrt(second_out / (1.0 - BETA_TWO**STEP)) + ADAM_EPS)
    )
    weight_out = weight_in - LEARN_RATE * (ratio + WEIGHT_DECAY * weight_in)
    return (weight_out, first_out, second_out)


def per_device(
    tokens,
    cotangent,
    kept_index,
    full_flag,
    labels,
    timesteps,
    class_table,
    heads_weight,
    heads_first,
    heads_second,
    output_weight,
    output_first,
    output_second,
    up_weight,
    up_first,
    up_second,
    down_weight,
    down_first,
    down_second,
    adaln_weight,
    adaln_first,
    adaln_second,
    mask_token,
    mask_first,
    mask_second,
):
    image_count, seq_length, model_width = tokens.shape
    section = lax.axis_index("section")
    core = lax.axis_index("core")
    plane = lax.axis_index("dp")
    chip = lax.axis_index("row") * 2 + section
    quarter = seq_length // 4
    shard = model_width // lax.axis_size("dp")
    columns = heads_weight.shape[-1]

    with jax.named_scope("weights_in"):
        half = shard // 2
        attn_parts = [heads_weight[0, 0], heads_weight[0, 1], heads_weight[0, 2], output_weight[0].T]

        def attn_rows(start):
            parts = [lax.dynamic_slice_in_dim(part, start, half, 0) for part in attn_parts]
            return jnp.concatenate(parts, axis=1).astype(BF)

        keep, given = send_shares(attn_rows, half, section, core)
        attn_width = keep.shape[1]
        if lax.axis_size("dp") == 4:
            cut = attn_width // 3
            first = keep[:, :cut]
            parts = [first] + [lax.ppermute(first, "dp", xor_route(4, m)) for m in (1, 2, 3)]
            given, *parts = tie(given, *parts)
            rest = gather_weight(jnp.concatenate([given, keep[:, cut:]], axis=1))
            keep_all = jnp.concatenate([assemble(parts, plane, core), rest[:, attn_width:]], axis=1)
        else:
            rest = gather_weight(jnp.concatenate([given, keep], axis=1))
            keep_all = rest[:, attn_width:]
        enc_attn, dec_attn = by_block(keep_all, rest[:, :attn_width], section)
        feed_pack = jnp.concatenate([up_weight[0], down_weight[0].T], axis=1).astype(BF)
        feed_pack, given = tie(feed_pack, given)

        def feed_rows(start):
            return lax.dynamic_slice_in_dim(feed_pack, start, half, 0)

        enc_feed_half, dec_feed_half = by_block(*send_shares(feed_rows, half, section, core), section)
        feed_width = feed_pack.shape[1] // 2
        enc_feed = gather_weight(enc_feed_half)

    with jax.named_scope("modulation"):
        codes = planes_gather(jnp.stack([labels, timesteps], axis=1))
        class_count = class_table.shape[0]
        label_hot = (codes[:, :1] == jnp.arange(class_count, dtype=jnp.int32)[None, :]).astype(BF)
        condition = mm(label_hot, class_table) + time_embed(codes[:, 1], model_width)
        cond_act = jax.nn.silu(condition).astype(BF)
        cond_rows = lax.dynamic_slice_in_dim(cond_act, plane * shard, shard, 1)
        adaln_part = planes_sum(mm(cond_rows, adaln_weight[0].astype(BF)))
        adaln_all = lax.all_gather(adaln_part, PLANE, axis=0, tiled=False)
        mod_all = lax.dynamic_index_in_dim(adaln_all, core, 1, keepdims=False)
        mod_all = mod_all.reshape(2, 6, model_width)
        enc_mod, dec_mod = mod_all[0], mod_all[1]

    def relative(values):
        parts = [
            lax.dynamic_slice_in_dim(values, (chip ^ offset) * quarter, quarter, 0)
            for offset in range(4)
        ]
        return jnp.concatenate(parts, axis=0)

    with jax.named_scope("placement"):
        image_tokens = lax.dynamic_index_in_dim(tokens, core, 0, keepdims=False)
        image_cot = relative(lax.dynamic_index_in_dim(cotangent, core, 0, keepdims=False))
        kept = relative(lax.dynamic_index_in_dim(kept_index, core, 0, keepdims=False))
        flag = lax.dynamic_index_in_dim(full_flag, core, 0, keepdims=False)
        plain_ids = jnp.arange(seq_length, dtype=jnp.int32)
        ids = ((plain_ids // quarter) ^ chip) * quarter + plain_ids % quarter
        live = ids < jnp.where(flag > 0, seq_length, seq_length // 2)
        place_plain = ((kept[:, None] == plain_ids[None, :]) & live[:, None]).astype(BF)
        place = ((kept[:, None] == ids[None, :]) & live[:, None]).astype(BF)
        live = live.astype(F32)
        uncovered = 1.0 - jnp.sum(place.astype(F32), axis=0)
        restore = (ids[:, None] == plain_ids[None, :]).astype(BF)
        enc_in = mm(place_plain, image_tokens)

    def feed_up(normed_b, feed):
        up_value = mm(normed_b, feed[:, :feed_width])
        return up_value, gelu_tanh(up_value).astype(BF)

    def feed_down(activated, feed):
        return sum_rows(mm_nt(activated, feed[:, feed_width:], BF))

    with jax.named_scope("encoder"):
        normed, stacked, attended, log_total, branch_a, hidden, normed_b = block_attention(
            enc_in, enc_mod, live, enc_attn, quarter
        )
        normed_b, dec_feed_half = tie(normed_b, dec_feed_half)
        dec_feed = gather_weight(dec_feed_half)
        enc_up_value, enc_act = feed_up(normed_b, enc_feed)
        branch_b = feed_down(enc_act, enc_feed)
        enc_branch_b = branch_b
        enc_out = (hidden + enc_mod[5][None] * branch_b) * live[:quarter, None]
        sent = gather_rows(enc_out.astype(BF))
        enc_attn_saved = (normed, stacked, attended, log_total)
        enc_feed_saved = (hidden, normed_b, branch_a)

    with jax.named_scope("decoder"):
        dec_in = mm_tn(place, sent) + uncovered[:, None] * mask_token[None, :]
        all_live = jnp.ones_like(live)
        normed, stacked, attended, log_total, branch_a, hidden, normed_b = block_attention(
            dec_in, dec_mod, all_live, dec_attn, quarter
        )
        dec_down_in = (dec_mod[5][None] * image_cot.astype(F32)).astype(BF)
        dec_act, dec_up_grad, dec_partial = feed_both(normed_b, dec_feed, dec_down_in)
        dec_attn_saved = (normed, stacked, attended, log_total)
        dec_feed_saved = (hidden, normed_b, branch_a)

    is_first = section == 0

    def both_images(mine):
        other = swap_cores(mine)
        pair = jnp.where(core == 0, jnp.stack([mine, other]), jnp.stack([other, mine]))
        return pair[None]

    ones = jnp.ones((1, model_width), F32)

    with jax.named_scope("decoder_back"):
        (hidden_grad, output_in, mods_b), dec_feed_sum = block_back_feed(
            dec_up_grad,
            dec_partial,
            dec_down_in,
            dec_act,
            image_cot[:quarter].astype(F32),
            dec_mod,
            dec_feed_saved,
            core,
            False,
        )
        output_in = gather_rows(output_in)
        parts, dec_attn_sum = block_back_attention(
            output_in,
            hidden_grad,
            dec_in[:quarter],
            dec_mod,
            all_live,
            dec_attn_saved,
            dec_attn,
            core,
        )
        parts, dec_feed_sum = tie(parts, dec_feed_sum)
        dec_grad, dec_low, mods_a = modulate_back(
            parts,
            dec_in[:quarter],
            hidden_grad,
            jnp.broadcast_to(uncovered[:quarter, None], hidden_grad.shape),
            dec_mod[1][None],
            ones,
        )
        mask_part = mods_a[2]
        dec_mods = (mods_a[0:2], mods_b[2:3], mods_b[0:2])
        dec_low = gather_rows(dec_low)

    with jax.named_scope("encoder_back"):
        enc_cot = mm(place, dec_low)
        down_in = (enc_mod[5][None] * enc_cot).astype(BF)
        act_grad = mm(down_in, enc_feed[:, feed_width:])
        up_grad = jax.vjp(gelu_tanh, enc_up_value)[1](act_grad)[0].astype(BF)
        partial = mm_nt(up_grad, enc_feed[:, :feed_width], BF)
        partial, dec_act = tie(partial, dec_act)
        (hidden_grad, output_in, mods_b), enc_feed_sum = block_back_feed(
            up_grad,
            partial,
            down_in,
            enc_act,
            enc_cot[:quarter],
            enc_mod,
            enc_feed_saved,
            core,
            True,
        )
        output_in, dec_attn_sum = tie(output_in, dec_attn_sum)
        output_in = gather_rows(output_in)
        branch_b = feed_down(dec_act, dec_feed)
        dec_out = dec_feed_saved[0] + dec_mod[5][None] * branch_b
        gate_grad = jnp.sum(image_cot[:quarter].astype(F32) * branch_b, axis=0, keepdims=True)
        dec_mods = dec_mods + (gate_grad,)
        enc_gate_grad = jnp.sum(enc_cot[:quarter] * enc_branch_b, axis=0, keepdims=True)
        dec_out = gather_rows(dec_out.astype(BF))
        layer_out = both_images(mm_tn(restore, jnp.where(is_first, sent, dec_out), BF))
        parts, enc_attn_sum = block_back_attention(
            output_in,
            hidden_grad,
            enc_in[:quarter],
            enc_mod,
            live,
            enc_attn_saved,
            enc_attn,
            core,
        )
        parts, enc_feed_sum, layer_out = tie(parts, enc_feed_sum, layer_out)
        _, enc_low, mods_a = modulate_back(
            parts, enc_in[:quarter], hidden_grad, hidden_grad, enc_mod[1][None], ones
        )
        enc_low = gather_rows(enc_low)
        enc_mods = (mods_a[0:2], mods_b[2:3], mods_b[0:2], enc_gate_grad)

    with jax.named_scope("modulation_back"):
        mod_parts = jnp.concatenate(enc_mods + dec_mods, axis=0)
        mod_parts = lax.all_to_all(mod_parts.reshape(8, -1), PLANE, 0, 0, tiled=True)
        mod_parts, enc_feed_sum, enc_low = tie(mod_parts, enc_feed_sum, enc_low)
        mod_grad = planes_gather(jnp.sum(mod_parts.reshape(4, 2, -1), axis=0))

    with jax.named_scope("outputs"):
        arrange = jnp.where(is_first, place_plain, restore)
        in_grads = both_images(mm_tn(arrange, jnp.where(is_first, enc_low, dec_low), BF))

    with jax.named_scope("returns"):
        keep, given = return_over_section(enc_feed_sum, dec_feed_sum, section)

    with jax.named_scope("modulation_back"):
        grad_adaln = lax.dot_general(
            cond_rows.astype(F32), mod_grad, (((0,), (0,)), ((), ())), precision=PRECISE
        )

    with jax.named_scope("norm"):
        square = jnp.sum(grad_adaln * grad_adaln)
        for part in (dec_attn_sum, dec_feed_sum, enc_feed_sum):
            square = square + squared(part)
        square, grad_adaln, keep, given, in_grads, dec_attn_sum, enc_attn_sum = tie(
            square, grad_adaln, keep, given, in_grads, dec_attn_sum, enc_attn_sum
        )
        feed_grad = return_over_core(keep, given, section, core)
        down_grad = turned(feed_grad[:, feed_width:])
        up_grad = feed_grad[:, :feed_width]
        square = square + squared(enc_attn_sum)
        totals = jnp.concatenate([mask_part, jnp.full((128,), square / 128.0, F32)])
        totals = sum_over(totals.reshape(1, -1), ("dp",))
        keep, given = return_over_section(enc_attn_sum, dec_attn_sum, section)
        totals, keep, given = tie(totals, keep, given)
        totals = sum_over(totals, ("row", "section", "core"))[0]
        attn_grad = return_over_core(keep, given, section, core)
        heads_grad = jnp.stack([attn_grad[:, i * columns : (i + 1) * columns] for i in range(3)])
        output_grad = turned(attn_grad[:, 3 * columns :])
        totals, heads_grad, output_grad, up_grad, down_grad = tie(
            totals, heads_grad, output_grad, up_grad, down_grad
        )
        mask_total = totals[:model_width]
        grad_norm = jnp.sqrt(jnp.sum(totals[model_width:]) + jnp.sum(mask_total * mask_total))
        factor = jnp.minimum(1.0, CLIP_NORM / (grad_norm + NORM_EPS))

    with jax.named_scope("update"):
        gradients = [
            part.astype(F32)[None] for part in (heads_grad, output_grad, up_grad, down_grad)
        ] + [grad_adaln[None]]
        masters = (heads_weight, output_weight, up_weight, down_weight, adaln_weight)
        firsts = (heads_first, output_first, up_first, down_first, adaln_first)
        seconds = (heads_second, output_second, up_second, down_second, adaln_second)
        updated = []
        for position in range(5):
            updated += adam_update(
                masters[position], firsts[position], seconds[position], gradients[position], factor
            )
        mask_next = adam_update(mask_token, mask_first, mask_second, mask_total, factor)

    return (layer_out, in_grads, *updated, *mask_next, grad_norm)


def solution(mesh):
    sizes = dict(mesh.shape)
    parted = Mesh(
        mesh.devices.reshape(sizes["section"], sizes["tensor"] // 2, 2, sizes["dp"]),
        ("section", "row", "core", "dp"),
    )
    tensor = ("row", "core")
    heads = P("section", None, "dp", tensor)
    tensor_dp = P("section", tensor, "dp")
    dp_tensor = P("section", "dp", tensor)
    weights = [heads] * 3 + [tensor_dp] * 3 + [dp_tensor] * 3 + [tensor_dp] * 3 + [dp_tensor] * 3
    images = P("dp", None, None)
    layers = P("section", "dp", None, None)
    return jax.shard_map(
        per_device,
        mesh=parted,
        in_specs=(
            images,
            images,
            P("dp", None),
            P("dp"),
            P("dp"),
            P("dp"),
            P(),
            *weights,
            P(),
            P(),
            P(),
        ),
        out_specs=(layers, layers, *weights, P(), P(), P(), P()),
        check_vma=False,
    )
```
